128 devices in a mesh: img: 32 (over y, x, z_hi), cen: 4 (over z_lo, core).
Axes of the slice: x: 4, y: 4, z: 4 (z_hi: 2, z_lo: 2; z = z_hi * 2 + z_lo), core: 2. Of those that a mesh axis runs over, the one named last changes fastest.
Arguments:
- embeddings: bfloat16 [32768, 1536], P(('img', 'cen')), may hold values from -8 to 8
- centroids: bfloat16 [4096, 1536], P('cen'), may hold values from -8 to 8
Outputs:
- new_centroids: float32 [4096, 1536], P(('cen', 'img'))
The draws below stay inside these ranges and needn't reach their ends.
All inputs are finite; a program needn't handle non-finite values.
Results may differ from the reference program's by a relative error of at most 0.0018.
Values may be sent and summed in bfloat16 or wider, within the bound.
A program may use at most 128 MiB of HBM per device.

```python
import math
import jax
import jax.numpy as jnp
from jax import lax

D = 1536
K = 4096
NROWS = 32768


def draw_embeddings(key, part):
    key = jax.random.fold_in(key, 1)
    first = jax.random.fold_in(key, 0)
    values = jnp.clip(jax.random.normal(first, (NROWS, D), jnp.float32), -4.0, 4.0)
    return values.astype(jnp.bfloat16)


def draw_centroids(key, part):
    key = jax.random.fold_in(key, 2)
    first = jax.random.fold_in(key, 0)
    values = jnp.clip(jax.random.normal(first, (K, D), jnp.float32), -4.0, 4.0)
    return values.astype(jnp.bfloat16)


def setup_inputs(seed: int = 0) -> dict:
    seeds = jax.random.split(jax.random.key(seed), 3)
    return {
        "embeddings": draw_embeddings(jax.random.fold_in(seeds[2], 71), 0),
        "centroids": draw_centroids(jax.random.fold_in(seeds[2], 71), 0),
    }


def reference(embeddings, centroids):
    scale = D ** (-0.5)
    width = math.gcd(NROWS, 4096)
    grouped = embeddings.reshape(NROWS // width, width, D)

    def accumulate(total, rows):
        scores = lax.dot_general(rows, centroids, (((1,), (1,)), ((), ())), preferred_element_type=jnp.float32) * scale
        row_max = lax.optimization_barrier(jnp.max(scores, axis=1, keepdims=True))
        expo = jnp.exp(scores - row_max)
        row_total = lax.optimization_barrier(jnp.sum(expo, axis=1, keepdims=True))
        resp = (expo / row_total).astype(jnp.bfloat16)
        part = lax.dot_general(resp, rows, (((0,), (0,)), ((), ())), preferred_element_type=jnp.float32)
        return (total + part, None)
    sums, unused = lax.scan(accumulate, jnp.zeros((K, D), jnp.float32), grouped)
    return sums * lax.rsqrt(lax.optimization_barrier(jnp.mean(sums * sums, axis=1, keepdims=True)) + 1e-06)
```

```python
import functools
import math

import jax
import jax.numpy as jnp
from jax import lax
from jax.experimental import pallas as pl
from jax.experimental.pallas import tpu as pltpu
from jax.sharding import PartitionSpec as P

MESH = pl.DeviceIdType.MESH
D = 1536
HALF = D // 2
KB = 1024
ROWS = 256
SCALE = D**-0.5 * math.log2(math.e)
WIDTHS = (512, 512, 256, 256)

HOME = 0
NEAR = 2
PASSED = 4
STATS = 6
RING = 8
FAR = 24
N_RECEIVE = 25
ROWS_OUT, STATS_OUT, RING_OUT, FAR_OUT, N_SEND = 0, 1, 2, 10, 11

POWER_SCALE = 2.0**13


def encode(v):
    u = v * POWER_SCALE
    return (u * u * (u * jnp.abs(u))).astype(jnp.bfloat16)


def decode(code):
    c = code.astype(jnp.float32)
    root = lax.rsqrt(lax.rsqrt(jnp.maximum(jnp.abs(c), 2.0**-126))) * (1.0 / POWER_SCALE)
    return jnp.where(c > 0.0, root, jnp.where(c < 0.0, -root, 0.0))


def kernel(e_hbm, c_hbm, out_ref, cen, rows, prob, resp, fac, st, st_in, early, rings, last, lsem, ssem, rsem):
    img, cpos = lax.axis_index("img"), lax.axis_index("cen")
    y, x, zh = lax.div(img, 8), lax.rem(lax.div(img, 2), 4), lax.rem(img, 2)
    zl, core = lax.div(cpos, 2), lax.rem(cpos, 2)
    z = zh * 2 + zl
    other = 1 - core

    def dev(yy, xx, zz, cc):
        return ((yy * 4 + xx) * 2 + lax.div(zz, 2), lax.rem(zz, 2) * 2 + cc)

    def step(v, by):
        return lax.rem(v + by, 4)

    up, down, far = step(z, 1), step(z, 3), step(z, 2)
    sib = dev(y, x, z, other)
    partners = [sib, dev(y, x, far, core)]
    partners += [dev(y, x, zz, cc) for zz in (up, down) for cc in (0, 1)]
    for zz in (z, far):
        partners += [dev(y, step(x, b), zz, core) for b in (1, 2, 3)]
        partners += [dev(step(y, b), x, zz, core) for b in (1, 2, 3)]

    def home(j, cc):
        return rows.at[pl.ds(pl.multiple_of(j * 512 + cc * 128, 128), 128)]

    def outer(j, cc):
        return rows.at[pl.ds(j * 512 + 256, 256), pl.ds(pl.multiple_of(cc * HALF, HALF), HALF)]

    loads = [pltpu.make_async_copy(e_hbm.at[pl.ds(j * 128, 128)], home(j, core), lsem.at[j]) for j in range(2)]
    loads.append(pltpu.make_async_copy(c_hbm, cen, lsem.at[2]))
    for c in loads:
        c.start()

    barrier = pltpu.get_barrier_semaphore()
    for who in partners:
        pl.semaphore_signal(barrier, inc=1, device_id=who, device_id_type=MESH)
    pl.semaphore_wait(barrier, len(partners))

    def copy(src, dst, out, into, who):
        return pltpu.make_async_remote_copy(
            src_ref=src, dst_ref=dst, send_sem=ssem.at[out], recv_sem=rsem.at[into], device_id=who, device_id_type=MESH
        )

    def send(src, dst, out, into, who):
        copy(src, dst, out, into, who).start()

    def arrived(ref, into):
        copy(ref, ref, 0, into, sib).wait_recv()

    def left(ref, out):
        copy(ref, ref, out, 0, sib).wait_send()

    z_to = step(z, 1 + 2 * core)
    for j in range(2):
        half = e_hbm.at[pl.ds(j * 128, 128)]
        for cc in range(2):
            cols = pl.ds(cc * HALF, HALF)
            to = rows.at[pl.ds(pl.multiple_of(j * 512 + 256 + core * 128, 128), 128), cols]
            send(e_hbm.at[pl.ds(j * 128, 128), cols], to, ROWS_OUT, NEAR + j, dev(y, x, z_to, cc))
        send(half, home(j, core), ROWS_OUT, HOME + j, sib)

    def forward(j):
        arrived(outer(j, core), NEAR + j)
        send(outer(j, core), outer(j, core), ROWS_OUT, PASSED + j, sib)

    def dots(ch, first, second):
        chunk = jnp.concatenate([first[...], second[...]], axis=0)
        m = None
        for kt in range(4):
            s = lax.dot_general(
                cen[kt * 256 : kt * 256 + 256, :],
                chunk,
                (((1,), (1,)), ((), ())),
                preferred_element_type=jnp.float32,
            )
            prob[ch, kt * 256 : kt * 256 + 256, :] = s
            top = jnp.max(s, axis=0, keepdims=True)
            m = top if m is None else jnp.maximum(m, top)
        return m

    def exps(ch, m):
        total = jnp.zeros((1, 256), jnp.float32)
        for kt in range(4):
            e = jnp.exp2((prob[ch, kt * 256 : kt * 256 + 256, :] - m) * SCALE)
            prob[ch, kt * 256 : kt * 256 + 256, :] = e
            total = total + jnp.sum(e, axis=0, keepdims=True)
        return total

    def note(j, slot, lanes, m, total):
        st[j, slot, 0:1, :] = m[:, lanes]
        st[j, slot, 1:2, :] = total[:, lanes]

    low, high = slice(0, 128), slice(128, 256)

    def note_home(ch, m, total):
        for j, lanes in enumerate((low, high)):
            note(j, 3 * ch, lanes, m, total)

    def tell(j):
        send(st.at[j], st_in.at[j, 0], STATS_OUT, STATS + j, sib)
        for cc in range(2):
            send(st.at[j, pl.ds(0, 2)], st_in.at[j, 1 + core, pl.ds(2, 2)], STATS_OUT, STATS + j, dev(y, x, up, cc))
            send(st.at[j, pl.ds(2, 2)], st_in.at[j, 1 + core, pl.ds(0, 2)], STATS_OUT, STATS + j, dev(y, x, down, cc))

    for c in loads:
        c.wait()
    m = dots(core, home(0, core), home(1, core))
    note_home(core, m, exps(core, m))
    for j in range(2):
        arrived(home(j, other), HOME + j)
    m = dots(other, home(0, other), home(1, other))
    forward(0)
    note_home(other, m, exps(other, m))
    for j in range(2):
        arrived(outer(j, other), PASSED + j)
        m = dots(2 + j, *(rows.at[j * 512 + 256 + d * 128 : j * 512 + 384 + d * 128] for d in range(2)))
        if j == 0:
            forward(1)
        total = exps(2 + j, m)
        note(j, 2, low, m, total)
        note(j, 1, high, m, total)
        tell(j)

    def respond(j):
        arrived(st_in.at[j], STATS + j)
        for slot, place in enumerate((0, 3, 2, 1)):
            mine = st[j, slot, 0:1, :]
            ms = [mine] + [st_in[j, k, slot, 0:1, :] for k in range(3)]
            ts = [st[j, slot, 1:2, :]] + [st_in[j, k, slot, 1:2, :] for k in range(3)]
            top = functools.reduce(jnp.maximum, ms)
            total = sum(t * jnp.exp2((m - top) * SCALE) for m, t in zip(ms, ts, strict=True))
            lane = j * 512 + place * 128
            fac[0:1, lane : lane + 128] = jnp.exp2((mine - top) * SCALE) / total
        for ch, lanes, at, width in ((0, j * 128, 0, 128), (1, j * 128, 128, 128), (2 + j, 0, 256, 256)):
            cols = slice(j * 512 + at, j * 512 + at + width)
            for kt in range(4):
                ks = slice(kt * 256, kt * 256 + 256)
                resp[ks, cols] = (prob[ch, ks, lanes : lanes + width] * fac[0:1, cols]).astype(jnp.bfloat16)

    def along(axis, by, zz=z):
        return dev(y, step(x, by), zz, core) if axis == 0 else dev(step(y, by), x, zz, core)

    place = (x, y)

    class Ring:
        def __init__(self, number):
            self.number, self.axis, self.width = number, number % 2, WIDTHS[number]
            self.at = sum(WIDTHS[:number])
            self.snd1, self.rcv1, self.next, self.part, self.snd2, self.rcv2 = rings[number]
            self.into, self.out = RING + 4 * number, RING_OUT + 2 * number

        def go1(self, kind, ways=(0, 1)):
            for way in ways:
                into = self.into + (kind > 0)
                send(self.snd1.at[kind, way], self.rcv1.at[kind, way], self.out, into, along(self.axis, 1 + 2 * way))

        def dots(self, by, first=0, last=1024):
            dest = step(place[self.axis], by)
            if self.axis == 0:
                parts = [resp[pl.ds(pl.multiple_of(s * 256 + dest * 64, 64), 64), first:last] for s in range(4)]
                left_side = jnp.concatenate(parts, axis=0)
            else:
                left_side = resp[pl.ds(pl.multiple_of(dest * 256, 256), 256), first:last]
            for c in range(0, self.width, 256):
                end = min(c + 256, self.width)
                right = rows[first:last, self.at + c : self.at + end]
                yield slice(c, end), jnp.dot(left_side, right, preferred_element_type=jnp.float32)

        def early(self, ref):
            for cols, v in self.dots(2, 0, 512):
                ref[:, cols] = v

        def far(self, ref=None):
            for cols, v in self.dots(2) if ref is None else self.dots(2, 512, 1024):
                if ref is not None:
                    v = v + ref[:, cols]
                for s in range(4):
                    for way in range(2):
                        self.snd1[0, way, s, :, cols] = v[s * 64 + way * 32 : s * 64 + way * 32 + 32].astype(jnp.bfloat16)

        def beside(self):
            for way in range(2):
                for cols, v in self.dots(1 + 2 * way):
                    for s in range(4):
                        split = [v[s * 64 + half * 32 : s * 64 + half * 32 + 32] for half in range(2)]
                        self.snd1[1, way, s, :, cols] = split[1 - way].astype(jnp.bfloat16)
                        self.next[way, s, :, cols] = split[way]
                self.go1(1, (way,))

        def own(self):
            for cols, v in self.dots(0):
                for s in range(4):
                    for half in range(2):
                        self.part[s, half, :, cols] = v[s * 64 + half * 32 : s * 64 + half * 32 + 32]

        def relay1(self):
            arrived(self.rcv1.at[0], self.into)
            for way in range(2):
                for s in range(4):
                    v = self.next[way, s] + self.rcv1[0, way, s].astype(jnp.float32)
                    self.snd1[2, way, s] = v.astype(jnp.bfloat16)
                self.go1(2, (way,))

        def arrive1(self):
            arrived(self.rcv1.at[pl.ds(1, 2)], self.into + 1)

        def settled(self, by, half):
            s = step(place[1 - self.axis], by)
            passed, plain = self.rcv1[2, half, s], self.rcv1[1, 1 - half, s]
            return self.part[s, half] + passed.astype(jnp.float32) + plain.astype(jnp.float32)

        def go2(self, way, kind):
            into = self.into + 2 + (kind > 0)
            to = along(1 - self.axis, 1 + 2 * way)
            send(self.snd2.at[way, kind], self.rcv2.at[way, kind], self.out + 1, into, to)

        def out2(self):
            for way in range(2):
                self.snd2[way, 0] = encode(self.settled(2, way))
                self.go2(way, 0)

        def beside2(self):
            for way in range(2):
                self.snd2[way, 1] = encode(self.settled(1 + 2 * way, 1 - way))
                self.go2(way, 1)

        def relay2(self):
            values = [self.settled(1 + 2 * way, way) for way in range(2)]
            arrived(self.rcv2.at[pl.ds(0, 2), 0], self.into + 2)
            for way in range(2):
                self.snd2[way, 2] = encode(values[way] + decode(self.rcv2[way, 0]))
                self.go2(way, 2)

        def out_straight(self):
            for across in (1, 0):
                for by in (2, 1, 3, 0):
                    if by or across:
                        slot = 2 * by + across - 1
                        self.snd2[slot] = encode(self.settled(by, zh + across * (1 - 2 * zh)))
                        to = along(1 - self.axis, by, far if across else z)
                        send(self.snd2.at[slot], self.rcv2.at[slot], self.out + 1, self.into + 2, to)

        def end_straight(self):
            mine = self.settled(0, zh)
            arrived(self.rcv2, self.into + 2)
            out_ref[:, self.at : self.at + self.width] = mine + sum(decode(self.rcv2[slot]) for slot in range(7))

        def end2(self):
            fin, zsnd = last[:2]
            cols = slice(self.at, self.at + self.width)
            values = [self.settled(0, half) for half in range(2)]
            arrived(self.rcv2.at[pl.ds(0, 2), pl.ds(1, 2)], self.into + 3)
            for half in range(2):
                fin[half, :, cols] = values[half] + decode(self.rcv2[half, 2]) + decode(self.rcv2[1 - half, 1])
            zsnd[:, cols] = encode(fin[1 - zh, :, cols])

    def out3():
        send(last[1], last[2], FAR_OUT, FAR, dev(y, x, far, core))

    def end3():
        fin, _, zrcv = last
        arrived(zrcv, FAR)
        out_ref[:, : 2 * WIDTHS[0]] = fin[zh] + decode(zrcv[...])

    a0, b0, a1, b1 = (Ring(n) for n in range(4))

    respond(0)
    a0.early(early.at[0])
    b0.early(early.at[1])
    respond(1)
    a0.far(early.at[0])
    a0.go1(0)
    b0.far(early.at[1])
    b0.go1(0)
    for r in (a0, b0):
        r.beside()
    for r in (a0, b0):
        r.own()
    for r in (a1, b1):
        r.far()
    for r in (a0, b0):
        r.relay1()
    for r in (a1, b1):
        r.go1(0)
    for r in (a1, b1):
        r.beside()
        r.own()
    left(rows.at[pl.ds(0, 768)], ROWS_OUT)
    left(st_in, STATS_OUT)
    for r in (a0, b0):
        r.arrive1()
        r.out2()
    for r in (a1, b1):
        r.relay1()
    for r in (a0, b0):
        r.beside2()
    for r in (a0, b0):
        r.relay2()
    for r in (a1, b1):
        r.arrive1()
        r.out_straight()
    for r in (a0, b0):
        r.end2()
    out3()
    for r in (a0, b0, a1, b1):
        left(r.snd1, r.out)
    for r in (a0, b0):
        left(r.snd2, r.out + 1)
    for r in (a1, b1):
        r.end_straight()
    end3()

    total = out_ref[...]
    norm = lax.rsqrt(jnp.sum(total * total, axis=1, keepdims=True) * (1.0 / D) + 1e-06)
    out_ref[...] = total * norm
    for r in (a1, b1):
        left(r.snd2, r.out + 1)
    left(last[1], FAR_OUT)


def ring_buffers(width):
    f32, bf16 = jnp.float32, jnp.bfloat16
    second = pltpu.VMEM((2, 3, 32, width) if width > 256 else (7, 32, width), bf16)
    return [
        pltpu.VMEM((3, 2, 4, 32, width), bf16),
        pltpu.VMEM((3, 2, 4, 32, width), bf16),
        pltpu.VMEM((2, 4, 32, width), f32),
        pltpu.VMEM((4, 2, 32, width), f32),
        second,
        second,
    ]


def per_device(embeddings, centroids):
    f32, bf16 = jnp.float32, jnp.bfloat16
    return pl.pallas_call(
        kernel,
        out_shape=pltpu.VMEM((32, D), f32),
        in_specs=[pl.BlockSpec(memory_space=pl.ANY)] * 2,
        out_specs=pl.BlockSpec(memory_space=pltpu.VMEM),
        scratch_shapes=[
            pltpu.VMEM((KB, D), bf16),
            pltpu.VMEM((4 * ROWS, D), bf16),
            pltpu.VMEM((4, KB, 256), f32),
            pltpu.VMEM((KB, 4 * ROWS), bf16),
            pltpu.VMEM((8, 4 * ROWS), f32),
            pltpu.VMEM((2, 4, 8, 128), f32),
            pltpu.VMEM((2, 3, 4, 8, 128), f32),
            pltpu.VMEM((2, 256, 512), f32),
            [ring_buffers(width) for width in WIDTHS],
            [
                pltpu.VMEM((2, 32, 2 * WIDTHS[0]), f32),
                pltpu.VMEM((32, 2 * WIDTHS[0]), bf16),
                pltpu.VMEM((32, 2 * WIDTHS[0]), bf16),
            ],
            pltpu.SemaphoreType.DMA((3,)),
            pltpu.SemaphoreType.DMA((N_SEND,)),
            pltpu.SemaphoreType.DMA((N_RECEIVE,)),
        ],
        compiler_params=pltpu.CompilerParams(collective_id=0, has_side_effects=True, vmem_limit_bytes=60 * 1024 * 1024),
        cost_estimate=pl.CostEstimate(flops=4 * KB * 4 * ROWS * D, bytes_accessed=5 * 1024 * 1024, transcendentals=KB * KB),
    )(embeddings, centroids)


def solution(mesh):
    placed = (P(("img", "cen"), None), P("cen", None))
    return jax.shard_map(per_device, mesh=mesh, in_specs=placed, out_specs=P(("cen", "img"), None), check_vma=False)
```

```python
import functools
import math

import jax
import jax.numpy as jnp
from jax import lax
from jax.experimental import pallas as pl
from jax.experimental.pallas import tpu as pltpu
from jax.sharding import PartitionSpec as P

MESH = pl.DeviceIdType.MESH
D = 1536
HALF = D // 2
KB = 1024
ROWS = 256
SCALE = D**-0.5 * math.log2(math.e)
WIDTHS = (512, 512, 256, 256)

HOME = 0
NEAR = 2
PASSED = 4
STATS = 6
RING = 8
FAR = 24
N_RECEIVE = 25
ROWS_OUT, STATS_OUT, RING_OUT, FAR_OUT, N_SEND = 0, 1, 2, 10, 11

POWER_SCALE = 2.0**13


def encode(v):
    u = v * POWER_SCALE
    return (u * u * (u * jnp.abs(u))).astype(jnp.bfloat16)


def decode(code):
    c = code.astype(jnp.float32)
    root = lax.rsqrt(lax.rsqrt(jnp.maximum(jnp.abs(c), 2.0**-126))) * (1.0 / POWER_SCALE)
    return jnp.where(c > 0.0, root, jnp.where(c < 0.0, -root, 0.0))


def kernel(e_hbm, c_hbm, out_ref, cen, rows, prob, resp, fac, st, st_in, early, rings, last, lsem, ssem, rsem):
    img, cpos = lax.axis_index("img"), lax.axis_index("cen")
    y, x, zh = lax.div(img, 8), lax.rem(lax.div(img, 2), 4), lax.rem(img, 2)
    zl, core = lax.div(cpos, 2), lax.rem(cpos, 2)
    z = zh * 2 + zl
    other = 1 - core

    def dev(yy, xx, zz, cc):
        return ((yy * 4 + xx) * 2 + lax.div(zz, 2), lax.rem(zz, 2) * 2 + cc)

    def step(v, by):
        return lax.rem(v + by, 4)

    up, down, far = step(z, 1), step(z, 3), step(z, 2)
    sib = dev(y, x, z, other)
    partners = [sib, dev(y, x, far, core)]
    partners += [dev(y, x, zz, cc) for zz in (up, down) for cc in (0, 1)]
    for zz in (z, far):
        partners += [dev(y, step(x, b), zz, core) for b in (1, 2, 3)]
        partners += [dev(step(y, b), x, zz, core) for b in (1, 2, 3)]

    def home(j, cc):
        return rows.at[pl.ds(pl.multiple_of(j * 512 + cc * 128, 128), 128)]

    def outer(j, cc):
        return rows.at[pl.ds(j * 512 + 256, 256), pl.ds(pl.multiple_of(cc * HALF, HALF), HALF)]

    loads = [pltpu.make_async_copy(e_hbm.at[pl.ds(j * 128, 128)], home(j, core), lsem.at[j]) for j in range(2)]
    quarters = [pl.ds(kt * 256, 256) for kt in range(4)]
    centroid_loads = [pltpu.make_async_copy(c_hbm.at[at], cen.at[at], lsem.at[2 + kt]) for kt, at in enumerate(quarters)]
    for c in loads + centroid_loads:
        c.start()

    barrier = pltpu.get_barrier_semaphore()
    for who in partners:
        pl.semaphore_signal(barrier, inc=1, device_id=who, device_id_type=MESH)
    pl.semaphore_wait(barrier, len(partners))

    def copy(src, dst, out, into, who):
        return pltpu.make_async_remote_copy(
            src_ref=src, dst_ref=dst, send_sem=ssem.at[out], recv_sem=rsem.at[into], device_id=who, device_id_type=MESH
        )

    def send(src, dst, out, into, who):
        copy(src, dst, out, into, who).start()

    def arrived(ref, into):
        copy(ref, ref, 0, into, sib).wait_recv()

    def left(ref, out):
        copy(ref, ref, out, 0, sib).wait_send()

    z_to = step(z, 1 + 2 * core)
    for j in range(2):
        half = e_hbm.at[pl.ds(j * 128, 128)]
        for cc in range(2):
            cols = pl.ds(cc * HALF, HALF)
            to = rows.at[pl.ds(pl.multiple_of(j * 512 + 256 + core * 128, 128), 128), cols]
            send(e_hbm.at[pl.ds(j * 128, 128), cols], to, ROWS_OUT, NEAR + j, dev(y, x, z_to, cc))
        send(half, home(j, core), ROWS_OUT, HOME + j, sib)

    def forward(j):
        arrived(outer(j, core), NEAR + j)
        send(outer(j, core), outer(j, core), ROWS_OUT, PASSED + j, sib)

    def dots(ch, first, second, waits=()):
        chunk = jnp.concatenate([first[...], second[...]], axis=0)
        m = None
        for kt in range(4):
            if waits:
                waits[kt].wait()
            s = lax.dot_general(
                cen[kt * 256 : kt * 256 + 256, :],
                chunk,
                (((1,), (1,)), ((), ())),
                preferred_element_type=jnp.float32,
            )
            prob[ch, kt * 256 : kt * 256 + 256, :] = s
            top = jnp.max(s, axis=0, keepdims=True)
            m = top if m is None else jnp.maximum(m, top)
        return m

    def exps(ch, m):
        total = jnp.zeros((1, 256), jnp.float32)
        for kt in range(4):
            e = jnp.exp2((prob[ch, kt * 256 : kt * 256 + 256, :] - m) * SCALE)
            prob[ch, kt * 256 : kt * 256 + 256, :] = e
            total = total + jnp.sum(e, axis=0, keepdims=True)
        return total

    def note(j, slot, lanes, m, total):
        st[j, slot, 0:1, :] = m[:, lanes]
        st[j, slot, 1:2, :] = total[:, lanes]

    low, high = slice(0, 128), slice(128, 256)

    def note_home(ch, m, total):
        for j, lanes in enumerate((low, high)):
            note(j, 3 * ch, lanes, m, total)

    def tell(j):
        send(st.at[j], st_in.at[j, 0], STATS_OUT, STATS + j, sib)
        for cc in range(2):
            send(st.at[j, pl.ds(0, 2)], st_in.at[j, 1 + core, pl.ds(2, 2)], STATS_OUT, STATS + j, dev(y, x, up, cc))
            send(st.at[j, pl.ds(2, 2)], st_in.at[j, 1 + core, pl.ds(0, 2)], STATS_OUT, STATS + j, dev(y, x, down, cc))

    for c in loads:
        c.wait()
    m = dots(core, home(0, core), home(1, core), centroid_loads)
    note_home(core, m, exps(core, m))
    for j in range(2):
        arrived(home(j, other), HOME + j)
    m = dots(other, home(0, other), home(1, other))
    forward(0)
    note_home(other, m, exps(other, m))
    for j in range(2):
        arrived(outer(j, other), PASSED + j)
        m = dots(2 + j, *(rows.at[j * 512 + 256 + d * 128 : j * 512 + 384 + d * 128] for d in range(2)))
        if j == 0:
            forward(1)
        total = exps(2 + j, m)
        note(j, 2, low, m, total)
        note(j, 1, high, m, total)
        tell(j)

    def respond(j):
        arrived(st_in.at[j], STATS + j)
        for slot, place in enumerate((0, 3, 2, 1)):
            mine = st[j, slot, 0:1, :]
            ms = [mine] + [st_in[j, k, slot, 0:1, :] for k in range(3)]
            ts = [st[j, slot, 1:2, :]] + [st_in[j, k, slot, 1:2, :] for k in range(3)]
            top = functools.reduce(jnp.maximum, ms)
            total = sum(t * jnp.exp2((m - top) * SCALE) for m, t in zip(ms, ts, strict=True))
            lane = j * 512 + place * 128
            fac[0:1, lane : lane + 128] = jnp.exp2((mine - top) * SCALE) / total
        for ch, lanes, at, width in ((0, j * 128, 0, 128), (1, j * 128, 128, 128), (2 + j, 0, 256, 256)):
            cols = slice(j * 512 + at, j * 512 + at + width)
            for kt in range(4):
                ks = slice(kt * 256, kt * 256 + 256)
                resp[ks, cols] = (prob[ch, ks, lanes : lanes + width] * fac[0:1, cols]).astype(jnp.bfloat16)

    def along(axis, by, zz=z):
        return dev(y, step(x, by), zz, core) if axis == 0 else dev(step(y, by), x, zz, core)

    place = (x, y)

    class Ring:
        def __init__(self, number):
            self.number, self.axis, self.width = number, number % 2, WIDTHS[number]
            self.at = sum(WIDTHS[:number])
            self.snd1, self.rcv1, self.next, self.part, self.snd2, self.rcv2 = rings[number]
            self.into, self.out = RING + 4 * number, RING_OUT + 2 * number

        def go1(self, kind, ways=(0, 1)):
            for way in ways:
                into = self.into + (kind > 0)
                send(self.snd1.at[kind, way], self.rcv1.at[kind, way], self.out, into, along(self.axis, 1 + 2 * way))

        def dots(self, by, first=0, last=1024):
            dest = step(place[self.axis], by)
            if self.axis == 0:
                parts = [resp[pl.ds(pl.multiple_of(s * 256 + dest * 64, 64), 64), first:last] for s in range(4)]
                left_side = jnp.concatenate(parts, axis=0)
            else:
                left_side = resp[pl.ds(pl.multiple_of(dest * 256, 256), 256), first:last]
            for c in range(0, self.width, 256):
                end = min(c + 256, self.width)
                right = rows[first:last, self.at + c : self.at + end]
                yield slice(c, end), jnp.dot(left_side, right, preferred_element_type=jnp.float32)

        def early(self, ref):
            for cols, v in self.dots(2, 0, 512):
                ref[:, cols] = v

        def far(self, ref=None):
            for cols, v in self.dots(2) if ref is None else self.dots(2, 512, 1024):
                if ref is not None:
                    v = v + ref[:, cols]
                for s in range(4):
                    for way in range(2):
                        self.snd1[0, way, s, :, cols] = v[s * 64 + way * 32 : s * 64 + way * 32 + 32].astype(jnp.bfloat16)

        def beside(self):
            for way in range(2):
                for cols, v in self.dots(1 + 2 * way):
                    for s in range(4):
                        split = [v[s * 64 + half * 32 : s * 64 + half * 32 + 32] for half in range(2)]
                        self.snd1[1, way, s, :, cols] = split[1 - way].astype(jnp.bfloat16)
                        self.next[way, s, :, cols] = split[way]
                self.go1(1, (way,))

        def own(self):
            for cols, v in self.dots(0):
                for s in range(4):
                    for half in range(2):
                        self.part[s, half, :, cols] = v[s * 64 + half * 32 : s * 64 + half * 32 + 32]

        def relay1(self):
            arrived(self.rcv1.at[0], self.into)
            for way in range(2):
                for s in range(4):
                    v = self.next[way, s] + self.rcv1[0, way, s].astype(jnp.float32)
                    self.snd1[2, way, s] = v.astype(jnp.bfloat16)
                self.go1(2, (way,))

        def arrive1(self):
            arrived(self.rcv1.at[pl.ds(1, 2)], self.into + 1)

        def settled(self, by, half):
            s = step(place[1 - self.axis], by)
            passed, plain = self.rcv1[2, half, s], self.rcv1[1, 1 - half, s]
            return self.part[s, half] + passed.astype(jnp.float32) + plain.astype(jnp.float32)

        def go2(self, way, kind):
            into = self.into + 2 + (kind > 0)
            to = along(1 - self.axis, 1 + 2 * way)
            send(self.snd2.at[way, kind], self.rcv2.at[way, kind], self.out + 1, into, to)

        def out2(self):
            for way in range(2):
                self.snd2[way, 0] = encode(self.settled(2, way))
                self.go2(way, 0)

        def beside2(self):
            for way in range(2):
                self.snd2[way, 1] = encode(self.settled(1 + 2 * way, 1 - way))
                self.go2(way, 1)

        def relay2(self):
            values = [self.settled(1 + 2 * way, way) for way in range(2)]
            arrived(self.rcv2.at[pl.ds(0, 2), 0], self.into + 2)
            for way in range(2):
                self.snd2[way, 2] = encode(values[way] + decode(self.rcv2[way, 0]))
                self.go2(way, 2)

        def out_straight(self):
            for across in (1, 0):
                for by in (2, 1, 3, 0):
                    if by or across:
                        slot = 2 * by + across - 1
                        self.snd2[slot] = encode(self.settled(by, zh + across * (1 - 2 * zh)))
                        to = along(1 - self.axis, by, far if across else z)
                        send(self.snd2.at[slot], self.rcv2.at[slot], self.out + 1, self.into + 2, to)

        def end_straight(self):
            mine = self.settled(0, zh)
            arrived(self.rcv2, self.into + 2)
            out_ref[:, self.at : self.at + self.width] = mine + sum(decode(self.rcv2[slot]) for slot in range(7))

        def end2(self):
            fin, zsnd = last[:2]
            cols = slice(self.at, self.at + self.width)
            values = [self.settled(0, half) for half in range(2)]
            arrived(self.rcv2.at[pl.ds(0, 2), pl.ds(1, 2)], self.into + 3)
            for half in range(2):
                fin[half, :, cols] = values[half] + decode(self.rcv2[half, 2]) + decode(self.rcv2[1 - half, 1])
            zsnd[:, cols] = encode(fin[1 - zh, :, cols])

    def out3():
        send(last[1], last[2], FAR_OUT, FAR, dev(y, x, far, core))

    def end3():
        fin, _, zrcv = last
        arrived(zrcv, FAR)
        out_ref[:, : 2 * WIDTHS[0]] = fin[zh] + decode(zrcv[...])

    a0, b0, a1, b1 = (Ring(n) for n in range(4))

    respond(0)
    a0.early(early.at[0])
    b0.early(early.at[1])
    respond(1)
    a0.far(early.at[0])
    a0.go1(0)
    b0.far(early.at[1])
    b0.go1(0)
    for r in (a0, b0):
        r.beside()
    for r in (a0, b0):
        r.own()
    for r in (a1, b1):
        r.far()
    for r in (a0, b0):
        r.relay1()
    for r in (a1, b1):
        r.go1(0)
    for r in (a1, b1):
        r.beside()
        r.own()
    left(rows.at[pl.ds(0, 768)], ROWS_OUT)
    left(st_in, STATS_OUT)
    for r in (a0, b0):
        r.arrive1()
        r.out2()
    for r in (a1, b1):
        r.relay1()
    for r in (a0, b0):
        r.beside2()
    for r in (a0, b0):
        r.relay2()
    for r in (a1, b1):
        r.arrive1()
        r.out_straight()
    for r in (a0, b0):
        r.end2()
    out3()
    for r in (a0, b0, a1, b1):
        left(r.snd1, r.out)
    for r in (a0, b0):
        left(r.snd2, r.out + 1)
    for r in (a1, b1):
        r.end_straight()
    end3()

    total = out_ref[...]
    norm = lax.rsqrt(jnp.sum(total * total, axis=1, keepdims=True) * (1.0 / D) + 1e-06)
    out_ref[...] = total * norm
    for r in (a1, b1):
        left(r.snd2, r.out + 1)
    left(last[1], FAR_OUT)


def ring_buffers(width):
    f32, bf16 = jnp.float32, jnp.bfloat16
    second = pltpu.VMEM((2, 3, 32, width) if width > 256 else (7, 32, width), bf16)
    return [
        pltpu.VMEM((3, 2, 4, 32, width), bf16),
        pltpu.VMEM((3, 2, 4, 32, width), bf16),
        pltpu.VMEM((2, 4, 32, width), f32),
        pltpu.VMEM((4, 2, 32, width), f32),
        second,
        second,
    ]


def per_device(embeddings, centroids):
    f32, bf16 = jnp.float32, jnp.bfloat16
    return pl.pallas_call(
        kernel,
        out_shape=pltpu.VMEM((32, D), f32),
        in_specs=[pl.BlockSpec(memory_space=pl.ANY)] * 2,
        out_specs=pl.BlockSpec(memory_space=pltpu.VMEM),
        scratch_shapes=[
            pltpu.VMEM((KB, D), bf16),
            pltpu.VMEM((4 * ROWS, D), bf16),
            pltpu.VMEM((4, KB, 256), f32),
            pltpu.VMEM((KB, 4 * ROWS), bf16),
            pltpu.VMEM((8, 4 * ROWS), f32),
            pltpu.VMEM((2, 4, 8, 128), f32),
            pltpu.VMEM((2, 3, 4, 8, 128), f32),
            pltpu.VMEM((2, 256, 512), f32),
            [ring_buffers(width) for width in WIDTHS],
            [
                pltpu.VMEM((2, 32, 2 * WIDTHS[0]), f32),
                pltpu.VMEM((32, 2 * WIDTHS[0]), bf16),
                pltpu.VMEM((32, 2 * WIDTHS[0]), bf16),
            ],
            pltpu.SemaphoreType.DMA((6,)),
            pltpu.SemaphoreType.DMA((N_SEND,)),
            pltpu.SemaphoreType.DMA((N_RECEIVE,)),
        ],
        compiler_params=pltpu.CompilerParams(collective_id=0, has_side_effects=True, vmem_limit_bytes=60 * 1024 * 1024),
        cost_estimate=pl.CostEstimate(flops=4 * KB * 4 * ROWS * D, bytes_accessed=5 * 1024 * 1024, transcendentals=KB * KB),
    )(embeddings, centroids)


def solution(mesh):
    placed = (P(("img", "cen"), None), P("cen", None))
    return jax.shard_map(per_device, mesh=mesh, in_specs=placed, out_specs=P(("cen", "img"), None), check_vma=False)
```

```python
import functools
import math

import jax
import jax.numpy as jnp
from jax import lax
from jax.experimental import pallas as pl
from jax.experimental.pallas import tpu as pltpu
from jax.sharding import PartitionSpec as P

MESH = pl.DeviceIdType.MESH
D = 1536
HALF = D // 2
KB = 1024
ROWS = 256
SCALE = D**-0.5 * math.log2(math.e)
SPLIT = (128, 96)
WIDTHS = (512, 512, 256, 256)

HOME = 0
NEAR = 2
PASSED = 4
STATS = 6
RING = 8
FAR = 24
BOTH = 25
N_RECEIVE = 26
ROWS_OUT, STATS_OUT, RING_OUT, FAR_OUT, N_SEND = 0, 1, 2, 10, 11

POWER_SCALE = 2.0**13


def encode(v):
    u = v * POWER_SCALE
    return (u * u * (u * jnp.abs(u))).astype(jnp.bfloat16)


def decode(code):
    c = code.astype(jnp.float32)
    root = lax.rsqrt(lax.rsqrt(jnp.maximum(jnp.abs(c), 2.0**-126))) * (1.0 / POWER_SCALE)
    return jnp.where(c > 0.0, root, jnp.where(c < 0.0, -root, 0.0))


def kernel(e_hbm, c_hbm, out_ref, cen, rows, prob, resp, fac, st, st_in, early, rings, last, lsem, ssem, rsem):
    img, cpos = lax.axis_index("img"), lax.axis_index("cen")
    y, x, zh = lax.div(img, 8), lax.rem(lax.div(img, 2), 4), lax.rem(img, 2)
    zl, core = lax.div(cpos, 2), lax.rem(cpos, 2)
    z = zh * 2 + zl
    other = 1 - core

    def dev(yy, xx, zz, cc):
        return ((yy * 4 + xx) * 2 + lax.div(zz, 2), lax.rem(zz, 2) * 2 + cc)

    def step(v, by):
        return lax.rem(v + by, 4)

    up, down, far = step(z, 1), step(z, 3), step(z, 2)
    sib = dev(y, x, z, other)
    partners = [sib, dev(y, x, far, core)]
    partners += [dev(y, x, zz, cc) for zz in (up, down) for cc in (0, 1)]
    for zz in (z, far):
        partners += [dev(y, step(x, b), zz, core) for b in (1, 2, 3)]
        partners += [dev(step(y, b), x, zz, core) for b in (1, 2, 3)]

    def home(j, cc):
        return rows.at[j * 4 + cc]

    def columns(cc):
        return pl.ds(pl.multiple_of(cc * HALF, HALF), HALF)

    def outer(j, cc):
        return rows.at[pl.ds(j * 4 + 2, 2), pl.ds(0, SPLIT[j]), columns(cc)]

    loads = [pltpu.make_async_copy(e_hbm.at[pl.ds(j * 128, 128)], home(j, core), lsem.at[j]) for j in range(2)]
    loads.append(pltpu.make_async_copy(c_hbm, cen, lsem.at[2]))
    for c in loads:
        c.start()

    barrier = pltpu.get_barrier_semaphore()
    for who in partners:
        pl.semaphore_signal(barrier, inc=1, device_id=who, device_id_type=MESH)
    pl.semaphore_wait(barrier, len(partners))

    def copy(src, dst, out, into, who):
        return pltpu.make_async_remote_copy(
            src_ref=src, dst_ref=dst, send_sem=ssem.at[out], recv_sem=rsem.at[into], device_id=who, device_id_type=MESH
        )

    def send(src, dst, out, into, who):
        copy(src, dst, out, into, who).start()

    def arrived(ref, into):
        copy(ref, ref, 0, into, sib).wait_recv()

    def left(ref, out):
        copy(ref, ref, out, 0, sib).wait_send()

    z_to = step(z, 1 + 2 * core)
    for j in range(2):
        for cc in range(2):
            src = e_hbm.at[pl.ds(j * 128, SPLIT[j]), columns(cc)]
            send(src, rows.at[j * 4 + 2 + core, pl.ds(0, SPLIT[j]), columns(cc)], ROWS_OUT, NEAR + j, dev(y, x, z_to, cc))
        send(e_hbm.at[pl.ds(j * 128, 128)], home(j, core), ROWS_OUT, HOME + j, sib)
    tail = pl.ds(SPLIT[1], 128 - SPLIT[1])
    for cc in range(2):
        src = e_hbm.at[pl.ds(128 + SPLIT[1], 128 - SPLIT[1])]
        send(src, rows.at[6 + core, tail], ROWS_OUT, BOTH, dev(y, x, z_to, cc))

    def forward(j):
        arrived(outer(j, core), NEAR + j)
        send(outer(j, core), outer(j, core), ROWS_OUT, PASSED + j, sib)

    def dots(ch, first, second):
        chunk = jnp.concatenate([first[...], second[...]], axis=0)
        m = None
        for kt in range(4):
            s = lax.dot_general(
                cen[kt * 256 : kt * 256 + 256, :],
                chunk,
                (((1,), (1,)), ((), ())),
                preferred_element_type=jnp.float32,
            )
            prob[ch, kt * 256 : kt * 256 + 256, :] = s
            top = jnp.max(s, axis=0, keepdims=True)
            m = top if m is None else jnp.maximum(m, top)
        return m

    def exps(ch, m):
        total = jnp.zeros((1, 256), jnp.float32)
        for kt in range(4):
            e = jnp.exp2((prob[ch, kt * 256 : kt * 256 + 256, :] - m) * SCALE)
            prob[ch, kt * 256 : kt * 256 + 256, :] = e
            total = total + jnp.sum(e, axis=0, keepdims=True)
        return total

    def note(j, slot, lanes, m, total):
        st[j, slot, 0:1, :] = m[:, lanes]
        st[j, slot, 1:2, :] = total[:, lanes]

    low, high = slice(0, 128), slice(128, 256)

    def note_home(ch, m, total):
        for j, lanes in enumerate((low, high)):
            note(j, 3 * ch, lanes, m, total)

    def tell(j):
        send(st.at[j], st_in.at[j, 0], STATS_OUT, STATS + j, sib)
        for cc in range(2):
            send(st.at[j, pl.ds(0, 2)], st_in.at[j, 1 + core, pl.ds(2, 2)], STATS_OUT, STATS + j, dev(y, x, up, cc))
            send(st.at[j, pl.ds(2, 2)], st_in.at[j, 1 + core, pl.ds(0, 2)], STATS_OUT, STATS + j, dev(y, x, down, cc))

    for c in loads:
        c.wait()
    m = dots(core, home(0, core), home(1, core))
    note_home(core, m, exps(core, m))
    for j in range(2):
        arrived(home(j, other), HOME + j)
    m = dots(other, home(0, other), home(1, other))
    forward(0)
    note_home(other, m, exps(other, m))
    for j in range(2):
        arrived(outer(j, other), PASSED + j)
        if j == 1:
            arrived(rows.at[pl.ds(6, 2), tail], BOTH)
        m = dots(2 + j, rows.at[j * 4 + 2], rows.at[j * 4 + 3])
        if j == 0:
            forward(1)
        total = exps(2 + j, m)
        note(j, 2, low, m, total)
        note(j, 1, high, m, total)
        tell(j)

    def respond(j):
        arrived(st_in.at[j], STATS + j)
        for slot, place in enumerate((0, 3, 2, 1)):
            mine = st[j, slot, 0:1, :]
            ms = [mine] + [st_in[j, k, slot, 0:1, :] for k in range(3)]
            ts = [st[j, slot, 1:2, :]] + [st_in[j, k, slot, 1:2, :] for k in range(3)]
            top = functools.reduce(jnp.maximum, ms)
            total = sum(t * jnp.exp2((m - top) * SCALE) for m, t in zip(ms, ts, strict=True))
            lane = j * 512 + place * 128
            fac[0:1, lane : lane + 128] = jnp.exp2((mine - top) * SCALE) / total
        for ch, lanes, at, width in ((0, j * 128, 0, 128), (1, j * 128, 128, 128), (2 + j, 0, 256, 256)):
            cols = slice(j * 512 + at, j * 512 + at + width)
            for kt in range(4):
                ks = slice(kt * 256, kt * 256 + 256)
                resp[ks, cols] = (prob[ch, ks, lanes : lanes + width] * fac[0:1, cols]).astype(jnp.bfloat16)

    def along(axis, by, zz=z):
        return dev(y, step(x, by), zz, core) if axis == 0 else dev(step(y, by), x, zz, core)

    place = (x, y)

    class Ring:
        def __init__(self, number):
            self.number, self.axis, self.width = number, number % 2, WIDTHS[number]
            self.at = sum(WIDTHS[:number])
            self.snd1, self.rcv1, self.next, self.part, self.snd2, self.rcv2 = rings[number]
            self.into, self.out = RING + 4 * number, RING_OUT + 2 * number

        def go1(self, kind, ways=(0, 1)):
            for way in ways:
                into = self.into + (kind > 0)
                send(self.snd1.at[kind, way], self.rcv1.at[kind, way], self.out, into, along(self.axis, 1 + 2 * way))

        def dots(self, by, first=0, last=1024):
            dest = step(place[self.axis], by)
            if self.axis == 0:
                parts = [resp[pl.ds(pl.multiple_of(s * 256 + dest * 64, 64), 64), first:last] for s in range(4)]
                left_side = jnp.concatenate(parts, axis=0)
            else:
                left_side = resp[pl.ds(pl.multiple_of(dest * 256, 256), 256), first:last]
            for c in range(0, self.width, 256):
                end = min(c + 256, self.width)
                right = rows[first // 128 : last // 128, :, self.at + c : self.at + end].reshape(last - first, end - c)
                yield slice(c, end), jnp.dot(left_side, right, preferred_element_type=jnp.float32)

        def early(self, ref):
            for cols, v in self.dots(2, 0, 512):
                ref[:, cols] = v

        def far(self, ref=None):
            for cols, v in self.dots(2) if ref is None else self.dots(2, 512, 1024):
                if ref is not None:
                    v = v + ref[:, cols]
                for s in range(4):
                    for way in range(2):
                        self.snd1[0, way, s, :, cols] = v[s * 64 + way * 32 : s * 64 + way * 32 + 32].astype(jnp.bfloat16)

        def beside(self):
            for way in range(2):
                for cols, v in self.dots(1 + 2 * way):
                    for s in range(4):
                        split = [v[s * 64 + half * 32 : s * 64 + half * 32 + 32] for half in range(2)]
                        self.snd1[1, way, s, :, cols] = split[1 - way].astype(jnp.bfloat16)
                        self.next[way, s, :, cols] = split[way]
                self.go1(1, (way,))

        def own(self):
            for cols, v in self.dots(0):
                for s in range(4):
                    for half in range(2):
                        self.part[s, half, :, cols] = v[s * 64 + half * 32 : s * 64 + half * 32 + 32]

        def relay1(self):
            arrived(self.rcv1.at[0], self.into)
            for way in range(2):
                for s in range(4):
                    v = self.next[way, s] + self.rcv1[0, way, s].astype(jnp.float32)
                    self.snd1[2, way, s] = v.astype(jnp.bfloat16)
                self.go1(2, (way,))

        def arrive1(self):
            arrived(self.rcv1.at[pl.ds(1, 2)], self.into + 1)

        def settled(self, by, half):
            s = step(place[1 - self.axis], by)
            passed, plain = self.rcv1[2, half, s], self.rcv1[1, 1 - half, s]
            return self.part[s, half] + passed.astype(jnp.float32) + plain.astype(jnp.float32)

        def go2(self, way, kind):
            into = self.into + 2 + (kind > 0)
            to = along(1 - self.axis, 1 + 2 * way)
            send(self.snd2.at[way, kind], self.rcv2.at[way, kind], self.out + 1, into, to)

        def out2(self):
            for way in range(2):
                self.snd2[way, 0] = encode(self.settled(2, way))
                self.go2(way, 0)

        def beside2(self):
            for way in range(2):
                self.snd2[way, 1] = encode(self.settled(1 + 2 * way, 1 - way))
                self.go2(way, 1)

        def relay2(self):
            values = [self.settled(1 + 2 * way, way) for way in range(2)]
            arrived(self.rcv2.at[pl.ds(0, 2), 0], self.into + 2)
            for way in range(2):
                self.snd2[way, 2] = encode(values[way] + decode(self.rcv2[way, 0]))
                self.go2(way, 2)

        def out_straight(self):
            for across in (1, 0):
                for by in (2, 1, 3, 0):
                    if by or across:
                        slot = 2 * by + across - 1
                        self.snd2[slot] = encode(self.settled(by, zh + across * (1 - 2 * zh)))
                        to = along(1 - self.axis, by, far if across else z)
                        send(self.snd2.at[slot], self.rcv2.at[slot], self.out + 1, self.into + 2, to)

        def end_straight(self):
            mine = self.settled(0, zh)
            arrived(self.rcv2, self.into + 2)
            out_ref[:, self.at : self.at + self.width] = mine + sum(decode(self.rcv2[slot]) for slot in range(7))

        def end2(self):
            fin, zsnd = last[:2]
            cols = slice(self.at, self.at + self.width)
            values = [self.settled(0, half) for half in range(2)]
            arrived(self.rcv2.at[pl.ds(0, 2), pl.ds(1, 2)], self.into + 3)
            for half in range(2):
                fin[half, :, cols] = values[half] + decode(self.rcv2[half, 2]) + decode(self.rcv2[1 - half, 1])
            zsnd[:, cols] = encode(fin[1 - zh, :, cols])

    def out3():
        send(last[1], last[2], FAR_OUT, FAR, dev(y, x, far, core))

    def end3():
        fin, _, zrcv = last
        arrived(zrcv, FAR)
        out_ref[:, : 2 * WIDTHS[0]] = fin[zh] + decode(zrcv[...])

    a0, b0, a1, b1 = (Ring(n) for n in range(4))

    respond(0)
    a0.early(early.at[0])
    b0.early(early.at[1])
    respond(1)
    a0.far(early.at[0])
    a0.go1(0)
    b0.far(early.at[1])
    b0.go1(0)
    for r in (a0, b0):
        r.beside()
    for r in (a0, b0):
        r.own()
    for r in (a1, b1):
        r.far()
    for r in (a0, b0):
        r.relay1()
    for r in (a1, b1):
        r.go1(0)
    for r in (a1, b1):
        r.beside()
        r.own()
    left(rows.at[pl.ds(0, 6)], ROWS_OUT)
    left(st_in, STATS_OUT)
    for r in (a0, b0):
        r.arrive1()
        r.out2()
    for r in (a1, b1):
        r.relay1()
    for r in (a0, b0):
        r.beside2()
    for r in (a0, b0):
        r.relay2()
    for r in (a1, b1):
        r.arrive1()
        r.out_straight()
    for r in (a0, b0):
        r.end2()
    out3()
    for r in (a0, b0, a1, b1):
        left(r.snd1, r.out)
    for r in (a0, b0):
        left(r.snd2, r.out + 1)
    for r in (a1, b1):
        r.end_straight()
    end3()

    total = out_ref[...]
    norm = lax.rsqrt(jnp.sum(total * total, axis=1, keepdims=True) * (1.0 / D) + 1e-06)
    out_ref[...] = total * norm
    for r in (a1, b1):
        left(r.snd2, r.out + 1)
    left(last[1], FAR_OUT)


def ring_buffers(width):
    f32, bf16 = jnp.float32, jnp.bfloat16
    second = pltpu.VMEM((2, 3, 32, width) if width > 256 else (7, 32, width), bf16)
    return [
        pltpu.VMEM((3, 2, 4, 32, width), bf16),
        pltpu.VMEM((3, 2, 4, 32, width), bf16),
        pltpu.VMEM((2, 4, 32, width), f32),
        pltpu.VMEM((4, 2, 32, width), f32),
        second,
        second,
    ]


def per_device(embeddings, centroids):
    f32, bf16 = jnp.float32, jnp.bfloat16
    return pl.pallas_call(
        kernel,
        out_shape=pltpu.VMEM((32, D), f32),
        in_specs=[pl.BlockSpec(memory_space=pl.ANY)] * 2,
        out_specs=pl.BlockSpec(memory_space=pltpu.VMEM),
        scratch_shapes=[
            pltpu.VMEM((KB, D), bf16),
            pltpu.VMEM((8, 128, D), bf16),
            pltpu.VMEM((4, KB, 256), f32),
            pltpu.VMEM((KB, 4 * ROWS), bf16),
            pltpu.VMEM((8, 4 * ROWS), f32),
            pltpu.VMEM((2, 4, 8, 128), f32),
            pltpu.VMEM((2, 3, 4, 8, 128), f32),
            pltpu.VMEM((2, 256, 512), f32),
            [ring_buffers(width) for width in WIDTHS],
            [
                pltpu.VMEM((2, 32, 2 * WIDTHS[0]), f32),
                pltpu.VMEM((32, 2 * WIDTHS[0]), bf16),
                pltpu.VMEM((32, 2 * WIDTHS[0]), bf16),
            ],
            pltpu.SemaphoreType.DMA((3,)),
            pltpu.SemaphoreType.DMA((N_SEND,)),
            pltpu.SemaphoreType.DMA((N_RECEIVE,)),
        ],
        compiler_params=pltpu.CompilerParams(collective_id=0, has_side_effects=True, vmem_limit_bytes=60 * 1024 * 1024),
        cost_estimate=pl.CostEstimate(flops=4 * KB * 4 * ROWS * D, bytes_accessed=5 * 1024 * 1024, transcendentals=KB * KB),
    )(embeddings, centroids)


def solution(mesh):
    placed = (P(("img", "cen"), None), P("cen", None))
    return jax.shard_map(per_device, mesh=mesh, in_specs=placed, out_specs=P(("cen", "img"), None), check_vma=False)
```

```python
import functools
import math

import jax
import jax.numpy as jnp
from jax import lax
from jax.experimental import pallas as pl
from jax.experimental.pallas import tpu as pltpu
from jax.sharding import PartitionSpec as P

MESH = pl.DeviceIdType.MESH
D = 1536
HALF = D // 2
KB = 1024
ROWS = 256
SCALE = D**-0.5 * math.log2(math.e)
SPLIT = (128, 96)
WIDTHS = (512, 512, 256, 256)

HOME = 0
NEAR = 2
PASSED = 4
STATS = 6
RING = 8
FAR = 24
BOTH = 25
N_RECEIVE = 26
ROWS_OUT, STATS_OUT, RING_OUT, FAR_OUT, N_SEND = 0, 1, 2, 10, 11

POWER_SCALE = 2.0**13


def encode(v):
    u = v * POWER_SCALE
    return (u * u * (u * jnp.abs(u))).astype(jnp.bfloat16)


def decode(code):
    c = code.astype(jnp.float32)
    root = lax.rsqrt(lax.rsqrt(jnp.maximum(jnp.abs(c), 2.0**-126))) * (1.0 / POWER_SCALE)
    return jnp.where(c > 0.0, root, jnp.where(c < 0.0, -root, 0.0))


def kernel(e_hbm, c_hbm, out_ref, cen, rows, prob, resp, fac, st, st_in, early, rings, last, lsem, ssem, rsem):
    img, cpos = lax.axis_index("img"), lax.axis_index("cen")
    y, x, zh = lax.div(img, 8), lax.rem(lax.div(img, 2), 4), lax.rem(img, 2)
    zl, core = lax.div(cpos, 2), lax.rem(cpos, 2)
    z = zh * 2 + zl
    other = 1 - core

    def dev(yy, xx, zz, cc):
        return ((yy * 4 + xx) * 2 + lax.div(zz, 2), lax.rem(zz, 2) * 2 + cc)

    def step(v, by):
        return lax.rem(v + by, 4)

    up, down, far = step(z, 1), step(z, 3), step(z, 2)
    sib = dev(y, x, z, other)
    partners = [dev(y, x, zz, cc) for zz in (up, down) for cc in (0, 1)] + [sib]
    partners += [dev(y, step(x, b), z, core) for b in (1, 3)]
    partners += [dev(step(y, b), x, z, core) for b in (1, 3)]

    def home(j, cc):
        return rows.at[j * 4 + cc]

    def columns(cc):
        return pl.ds(pl.multiple_of(cc * HALF, HALF), HALF)

    def outer(j, cc):
        return rows.at[pl.ds(j * 4 + 2, 2), pl.ds(0, SPLIT[j]), columns(cc)]

    loads = [pltpu.make_async_copy(e_hbm.at[pl.ds(j * 128, 128)], home(j, core), lsem.at[j]) for j in range(2)]
    loads.append(pltpu.make_async_copy(c_hbm, cen, lsem.at[2]))
    for c in loads:
        c.start()

    barrier = pltpu.get_barrier_semaphore()
    for who in partners:
        pl.semaphore_signal(barrier, inc=1, device_id=who, device_id_type=MESH)
    pl.semaphore_wait(barrier, len(partners))

    def copy(src, dst, out, into, who):
        return pltpu.make_async_remote_copy(
            src_ref=src, dst_ref=dst, send_sem=ssem.at[out], recv_sem=rsem.at[into], device_id=who, device_id_type=MESH
        )

    def send(src, dst, out, into, who):
        copy(src, dst, out, into, who).start()

    def arrived(ref, into):
        copy(ref, ref, 0, into, sib).wait_recv()

    def left(ref, out):
        copy(ref, ref, out, 0, sib).wait_send()

    z_to = step(z, 1 + 2 * core)
    for j in range(2):
        for cc in range(2):
            src = e_hbm.at[pl.ds(j * 128, SPLIT[j]), columns(cc)]
            send(src, rows.at[j * 4 + 2 + core, pl.ds(0, SPLIT[j]), columns(cc)], ROWS_OUT, NEAR + j, dev(y, x, z_to, cc))
        send(e_hbm.at[pl.ds(j * 128, 128)], home(j, core), ROWS_OUT, HOME + j, sib)
    tail = pl.ds(SPLIT[1], 128 - SPLIT[1])
    for cc in range(2):
        src = e_hbm.at[pl.ds(128 + SPLIT[1], 128 - SPLIT[1])]
        send(src, rows.at[6 + core, tail], ROWS_OUT, BOTH, dev(y, x, z_to, cc))

    def forward(j):
        arrived(outer(j, core), NEAR + j)
        send(outer(j, core), outer(j, core), ROWS_OUT, PASSED + j, sib)

    def dots(ch, first, second):
        chunk = jnp.concatenate([first[...], second[...]], axis=0)
        m = None
        for kt in range(4):
            s = lax.dot_general(
                cen[kt * 256 : kt * 256 + 256, :],
                chunk,
                (((1,), (1,)), ((), ())),
                preferred_element_type=jnp.float32,
            )
            prob[ch, kt * 256 : kt * 256 + 256, :] = s
            top = jnp.max(s, axis=0, keepdims=True)
            m = top if m is None else jnp.maximum(m, top)
        return m

    def exps(ch, m):
        total = jnp.zeros((1, 256), jnp.float32)
        for kt in range(4):
            e = jnp.exp2((prob[ch, kt * 256 : kt * 256 + 256, :] - m) * SCALE)
            prob[ch, kt * 256 : kt * 256 + 256, :] = e
            total = total + jnp.sum(e, axis=0, keepdims=True)
        return total

    def note(j, slot, lanes, m, total):
        st[j, slot, 0:1, :] = m[:, lanes]
        st[j, slot, 1:2, :] = total[:, lanes]

    low, high = slice(0, 128), slice(128, 256)

    def note_home(ch, m, total):
        for j, lanes in enumerate((low, high)):
            note(j, 3 * ch, lanes, m, total)

    def tell(j):
        for cc in range(2):
            send(st.at[j, pl.ds(0, 2)], st_in.at[j, 1 + core, pl.ds(2, 2)], STATS_OUT, STATS + j, dev(y, x, up, cc))
            send(st.at[j, pl.ds(2, 2)], st_in.at[j, 1 + core, pl.ds(0, 2)], STATS_OUT, STATS + j, dev(y, x, down, cc))
        send(st.at[j], st_in.at[j, 0], STATS_OUT, STATS + j, sib)

    for c in loads:
        c.wait()
    m = dots(core, home(0, core), home(1, core))
    note_home(core, m, exps(core, m))
    for j in range(2):
        arrived(home(j, other), HOME + j)
    m = dots(other, home(0, other), home(1, other))
    forward(0)
    note_home(other, m, exps(other, m))
    for j in range(2):
        arrived(outer(j, other), PASSED + j)
        if j == 1:
            arrived(rows.at[pl.ds(6, 2), tail], BOTH)
        m = dots(2 + j, rows.at[j * 4 + 2], rows.at[j * 4 + 3])
        if j == 0:
            forward(1)
        total = exps(2 + j, m)
        note(j, 2, low, m, total)
        note(j, 1, high, m, total)
        tell(j)

    def respond(j):
        arrived(st_in.at[j], STATS + j)
        for slot, place in enumerate((0, 3, 2, 1)):
            mine = st[j, slot, 0:1, :]
            ms = [mine] + [st_in[j, k, slot, 0:1, :] for k in range(3)]
            ts = [st[j, slot, 1:2, :]] + [st_in[j, k, slot, 1:2, :] for k in range(3)]
            top = functools.reduce(jnp.maximum, ms)
            total = sum(t * jnp.exp2((m - top) * SCALE) for m, t in zip(ms, ts, strict=True))
            lane = j * 512 + place * 128
            fac[0:1, lane : lane + 128] = jnp.exp2((mine - top) * SCALE) / total
        for ch, lanes, at, width in ((0, j * 128, 0, 128), (1, j * 128, 128, 128), (2 + j, 0, 256, 256)):
            cols = slice(j * 512 + at, j * 512 + at + width)
            for kt in range(4):
                ks = slice(kt * 256, kt * 256 + 256)
                resp[ks, cols] = (prob[ch, ks, lanes : lanes + width] * fac[0:1, cols]).astype(jnp.bfloat16)

    def along(axis, by, zz=z):
        return dev(y, step(x, by), zz, core) if axis == 0 else dev(step(y, by), x, zz, core)

    place = (x, y)

    class Ring:
        def __init__(self, number):
            self.number, self.axis, self.width = number, number % 2, WIDTHS[number]
            self.at = sum(WIDTHS[:number])
            self.snd1, self.rcv1, self.next, self.part, self.snd2, self.rcv2 = rings[number]
            self.into, self.out = RING + 4 * number, RING_OUT + 2 * number

        def go1(self, kind, ways=(0, 1)):
            for way in ways:
                into = self.into + (kind > 0)
                send(self.snd1.at[kind, way], self.rcv1.at[kind, way], self.out, into, along(self.axis, 1 + 2 * way))

        def dots(self, by, first=0, last=1024):
            dest = step(place[self.axis], by)
            if self.axis == 0:
                parts = [resp[pl.ds(pl.multiple_of(s * 256 + dest * 64, 64), 64), first:last] for s in range(4)]
                left_side = jnp.concatenate(parts, axis=0)
            else:
                left_side = resp[pl.ds(pl.multiple_of(dest * 256, 256), 256), first:last]
            for c in range(0, self.width, 256):
                end = min(c + 256, self.width)
                right = rows[first // 128 : last // 128, :, self.at + c : self.at + end].reshape(last - first, end - c)
                yield slice(c, end), jnp.dot(left_side, right, preferred_element_type=jnp.float32)

        def early(self, ref):
            for cols, v in self.dots(2, 0, 512):
                ref[:, cols] = v

        def far(self, ref=None):
            for cols, v in self.dots(2) if ref is None else self.dots(2, 512, 1024):
                if ref is not None:
                    v = v + ref[:, cols]
                for s in range(4):
                    for way in range(2):
                        self.snd1[0, way, s, :, cols] = v[s * 64 + way * 32 : s * 64 + way * 32 + 32].astype(jnp.bfloat16)

        def beside(self):
            for way in range(2):
                for cols, v in self.dots(1 + 2 * way):
                    for s in range(4):
                        split = [v[s * 64 + half * 32 : s * 64 + half * 32 + 32] for half in range(2)]
                        self.snd1[1, way, s, :, cols] = split[1 - way].astype(jnp.bfloat16)
                        self.next[way, s, :, cols] = split[way]
                self.go1(1, (way,))

        def own(self):
            for cols, v in self.dots(0):
                for s in range(4):
                    for half in range(2):
                        self.part[s, half, :, cols] = v[s * 64 + half * 32 : s * 64 + half * 32 + 32]

        def relay1(self):
            arrived(self.rcv1.at[0], self.into)
            for way in range(2):
                for s in range(4):
                    v = self.next[way, s] + self.rcv1[0, way, s].astype(jnp.float32)
                    self.snd1[2, way, s] = v.astype(jnp.bfloat16)
                self.go1(2, (way,))

        def arrive1(self):
            arrived(self.rcv1.at[pl.ds(1, 2)], self.into + 1)

        def settled(self, by, half):
            s = step(place[1 - self.axis], by)
            passed, plain = self.rcv1[2, half, s], self.rcv1[1, 1 - half, s]
            return self.part[s, half] + passed.astype(jnp.float32) + plain.astype(jnp.float32)

        def go2(self, way, kind):
            into = self.into + 2 + (kind > 0)
            to = along(1 - self.axis, 1 + 2 * way)
            send(self.snd2.at[way, kind], self.rcv2.at[way, kind], self.out + 1, into, to)

        def out2(self):
            for way in range(2):
                self.snd2[way, 0] = encode(self.settled(2, way))
                self.go2(way, 0)

        def beside2(self):
            for way in range(2):
                self.snd2[way, 1] = encode(self.settled(1 + 2 * way, 1 - way))
                self.go2(way, 1)

        def relay2(self):
            values = [self.settled(1 + 2 * way, way) for way in range(2)]
            arrived(self.rcv2.at[pl.ds(0, 2), 0], self.into + 2)
            for way in range(2):
                self.snd2[way, 2] = encode(values[way] + decode(self.rcv2[way, 0]))
                self.go2(way, 2)

        def out_straight(self):
            for across in (1, 0):
                for by in (2, 1, 3, 0):
                    if by or across:
                        slot = 2 * by + across - 1
                        self.snd2[slot] = encode(self.settled(by, zh + across * (1 - 2 * zh)))
                        to = along(1 - self.axis, by, far if across else z)
                        send(self.snd2.at[slot], self.rcv2.at[slot], self.out + 1, self.into + 2, to)

        def end_straight(self):
            mine = self.settled(0, zh)
            arrived(self.rcv2, self.into + 2)
            out_ref[:, self.at : self.at + self.width] = mine + sum(decode(self.rcv2[slot]) for slot in range(7))

        def end2(self):
            fin, zsnd = last[:2]
            cols = slice(self.at, self.at + self.width)
            values = [self.settled(0, half) for half in range(2)]
            arrived(self.rcv2.at[pl.ds(0, 2), pl.ds(1, 2)], self.into + 3)
            for half in range(2):
                fin[half, :, cols] = values[half] + decode(self.rcv2[half, 2]) + decode(self.rcv2[1 - half, 1])
            zsnd[:, cols] = encode(fin[1 - zh, :, cols])

    def out3():
        send(last[1], last[2], FAR_OUT, FAR, dev(y, x, far, core))

    def end3():
        fin, _, zrcv = last
        arrived(zrcv, FAR)
        out_ref[:, : 2 * WIDTHS[0]] = fin[zh] + decode(zrcv[...])

    a0, b0, a1, b1 = (Ring(n) for n in range(4))

    respond(0)
    a0.early(early.at[0])
    b0.early(early.at[1])
    respond(1)
    a0.far(early.at[0])
    a0.go1(0)
    b0.far(early.at[1])
    b0.go1(0)
    for r in (a0, b0):
        r.beside()
    for r in (a0, b0):
        r.own()
    for r in (a1, b1):
        r.far()
    for r in (a0, b0):
        r.relay1()
    for r in (a1, b1):
        r.go1(0)
    for r in (a1, b1):
        r.beside()
        r.own()
    left(rows.at[pl.ds(0, 6)], ROWS_OUT)
    left(st_in, STATS_OUT)
    for r in (a0, b0):
        r.arrive1()
        r.out2()
    for r in (a1, b1):
        r.relay1()
    for r in (a0, b0):
        r.beside2()
    for r in (a0, b0):
        r.relay2()
    for r in (a1, b1):
        r.arrive1()
        r.out_straight()
    for r in (a0, b0):
        r.end2()
    out3()
    for r in (a0, b0, a1, b1):
        left(r.snd1, r.out)
    for r in (a0, b0):
        left(r.snd2, r.out + 1)
    for r in (a1, b1):
        r.end_straight()
    end3()

    total = out_ref[...]
    norm = lax.rsqrt(jnp.sum(total * total, axis=1, keepdims=True) * (1.0 / D) + 1e-06)
    out_ref[...] = total * norm
    for r in (a1, b1):
        left(r.snd2, r.out + 1)
    left(last[1], FAR_OUT)


def ring_buffers(width):
    f32, bf16 = jnp.float32, jnp.bfloat16
    second = pltpu.VMEM((2, 3, 32, width) if width > 256 else (7, 32, width), bf16)
    return [
        pltpu.VMEM((3, 2, 4, 32, width), bf16),
        pltpu.VMEM((3, 2, 4, 32, width), bf16),
        pltpu.VMEM((2, 4, 32, width), f32),
        pltpu.VMEM((4, 2, 32, width), f32),
        second,
        second,
    ]


def per_device(embeddings, centroids):
    f32, bf16 = jnp.float32, jnp.bfloat16
    return pl.pallas_call(
        kernel,
        out_shape=pltpu.VMEM((32, D), f32),
        in_specs=[pl.BlockSpec(memory_space=pl.ANY)] * 2,
        out_specs=pl.BlockSpec(memory_space=pltpu.VMEM),
        scratch_shapes=[
            pltpu.VMEM((KB, D), bf16),
            pltpu.VMEM((8, 128, D), bf16),
            pltpu.VMEM((4, KB, 256), f32),
            pltpu.VMEM((KB, 4 * ROWS), bf16),
            pltpu.VMEM((8, 4 * ROWS), f32),
            pltpu.VMEM((2, 4, 8, 128), f32),
            pltpu.VMEM((2, 3, 4, 8, 128), f32),
            pltpu.VMEM((2, 256, 512), f32),
            [ring_buffers(width) for width in WIDTHS],
            [
                pltpu.VMEM((2, 32, 2 * WIDTHS[0]), f32),
                pltpu.VMEM((32, 2 * WIDTHS[0]), bf16),
                pltpu.VMEM((32, 2 * WIDTHS[0]), bf16),
            ],
            pltpu.SemaphoreType.DMA((3,)),
            pltpu.SemaphoreType.DMA((N_SEND,)),
            pltpu.SemaphoreType.DMA((N_RECEIVE,)),
        ],
        compiler_params=pltpu.CompilerParams(collective_id=0, has_side_effects=True, vmem_limit_bytes=60 * 1024 * 1024),
        cost_estimate=pl.CostEstimate(flops=4 * KB * 4 * ROWS * D, bytes_accessed=5 * 1024 * 1024, transcendentals=KB * KB),
    )(embeddings, centroids)


def solution(mesh):
    placed = (P(("img", "cen"), None), P("cen", None))
    return jax.shard_map(per_device, mesh=mesh, in_specs=placed, out_specs=P(("cen", "img"), None), check_vma=False)
```

```python
import functools
import math

import jax
import jax.numpy as jnp
from jax import lax
from jax.experimental import pallas as pl
from jax.experimental.pallas import tpu as pltpu
from jax.sharding import PartitionSpec as P

MESH = pl.DeviceIdType.MESH
D = 1536
HALF = D // 2
KB = 1024
ROWS = 256
SCALE = D**-0.5 * math.log2(math.e)
SPLIT = (128, 96)
WIDTHS = (512, 512, 256, 256)

HOME = 0
NEAR = 2
PASSED = 4
STATS = 6
RING = 8
FAR = 24
BOTH = 25
N_RECEIVE = 26
ROWS_OUT, STATS_OUT, RING_OUT, FAR_OUT, N_SEND = 0, 1, 2, 10, 11

POWER_SCALE = 2.0**13


def encode(v):
    u = v * POWER_SCALE
    return (u * u * (u * jnp.abs(u))).astype(jnp.bfloat16)


def decode(code):
    c = code.astype(jnp.float32)
    root = lax.rsqrt(lax.rsqrt(jnp.maximum(jnp.abs(c), 2.0**-126))) * (1.0 / POWER_SCALE)
    return jnp.where(c > 0.0, root, jnp.where(c < 0.0, -root, 0.0))


def kernel(e_hbm, c_hbm, out_ref, cen, rows, prob, resp, fac, st, st_in, early, rings, last, lsem, ssem, rsem):
    img, cpos = lax.axis_index("img"), lax.axis_index("cen")
    y, x, zh = lax.div(img, 8), lax.rem(lax.div(img, 2), 4), lax.rem(img, 2)
    zl, core = lax.div(cpos, 2), lax.rem(cpos, 2)
    z = zh * 2 + zl
    other = 1 - core

    def dev(yy, xx, zz, cc):
        return ((yy * 4 + xx) * 2 + lax.div(zz, 2), lax.rem(zz, 2) * 2 + cc)

    def step(v, by):
        return lax.rem(v + by, 4)

    up, down, far = step(z, 1), step(z, 3), step(z, 2)
    sib = dev(y, x, z, other)
    partners = [dev(y, x, zz, cc) for zz in (up, down) for cc in (0, 1)] + [sib]
    partners += [dev(y, step(x, b), z, core) for b in (1, 3)]
    partners += [dev(step(y, b), x, z, core) for b in (1, 3)]

    barrier = pltpu.get_barrier_semaphore()
    for who in partners:
        pl.semaphore_signal(barrier, inc=1, device_id=who, device_id_type=MESH)

    def home(j, cc):
        return rows.at[j * 4 + cc]

    def columns(cc):
        return pl.ds(pl.multiple_of(cc * HALF, HALF), HALF)

    def outer(j, cc):
        return rows.at[pl.ds(j * 4 + 2, 2), pl.ds(0, SPLIT[j]), columns(cc)]

    loads = [pltpu.make_async_copy(e_hbm.at[pl.ds(j * 128, 128)], home(j, core), lsem.at[j]) for j in range(2)]
    loads.append(pltpu.make_async_copy(c_hbm, cen, lsem.at[2]))
    for c in loads:
        c.start()

    pl.semaphore_wait(barrier, len(partners))

    def copy(src, dst, out, into, who):
        return pltpu.make_async_remote_copy(
            src_ref=src, dst_ref=dst, send_sem=ssem.at[out], recv_sem=rsem.at[into], device_id=who, device_id_type=MESH
        )

    def send(src, dst, out, into, who):
        copy(src, dst, out, into, who).start()

    def arrived(ref, into):
        copy(ref, ref, 0, into, sib).wait_recv()

    def left(ref, out):
        copy(ref, ref, out, 0, sib).wait_send()

    z_to = step(z, 1 + 2 * core)
    for j in range(2):
        for cc in range(2):
            src = e_hbm.at[pl.ds(j * 128, SPLIT[j]), columns(cc)]
            send(src, rows.at[j * 4 + 2 + core, pl.ds(0, SPLIT[j]), columns(cc)], ROWS_OUT, NEAR + j, dev(y, x, z_to, cc))
        if j == 0:
            for half in range(2):
                send(e_hbm.at[pl.ds(half * 128, 128)], home(half, core), ROWS_OUT, HOME + half, sib)
    tail = pl.ds(SPLIT[1], 128 - SPLIT[1])
    for cc in range(2):
        src = e_hbm.at[pl.ds(128 + SPLIT[1], 128 - SPLIT[1])]
        send(src, rows.at[6 + core, tail], ROWS_OUT, BOTH, dev(y, x, z_to, cc))

    def forward(j):
        arrived(outer(j, core), NEAR + j)
        send(outer(j, core), outer(j, core), ROWS_OUT, PASSED + j, sib)

    def dots(ch, first, second):
        chunk = jnp.concatenate([first[...], second[...]], axis=0)
        m = None
        for kt in range(4):
            s = lax.dot_general(
                cen[kt * 256 : kt * 256 + 256, :],
                chunk,
                (((1,), (1,)), ((), ())),
                preferred_element_type=jnp.float32,
            )
            prob[ch, kt * 256 : kt * 256 + 256, :] = s
            top = jnp.max(s, axis=0, keepdims=True)
            m = top if m is None else jnp.maximum(m, top)
        return m

    def exps(ch, m):
        total = jnp.zeros((1, 256), jnp.float32)
        for kt in range(4):
            e = jnp.exp2((prob[ch, kt * 256 : kt * 256 + 256, :] - m) * SCALE)
            prob[ch, kt * 256 : kt * 256 + 256, :] = e
            total = total + jnp.sum(e, axis=0, keepdims=True)
        return total

    def note(j, slot, lanes, m, total):
        st[j, slot, 0:1, :] = m[:, lanes]
        st[j, slot, 1:2, :] = total[:, lanes]

    low, high = slice(0, 128), slice(128, 256)

    def note_home(ch, m, total):
        for j, lanes in enumerate((low, high)):
            note(j, 3 * ch, lanes, m, total)

    def tell(j):
        for cc in range(2):
            send(st.at[j, pl.ds(0, 2)], st_in.at[j, 1 + core, pl.ds(2, 2)], STATS_OUT, STATS + j, dev(y, x, up, cc))
            send(st.at[j, pl.ds(2, 2)], st_in.at[j, 1 + core, pl.ds(0, 2)], STATS_OUT, STATS + j, dev(y, x, down, cc))
        send(st.at[j], st_in.at[j, 0], STATS_OUT, STATS + j, sib)

    for c in loads:
        c.wait()
    m = dots(core, home(0, core), home(1, core))
    note_home(core, m, exps(core, m))
    for j in range(2):
        arrived(home(j, other), HOME + j)
    m = dots(other, home(0, other), home(1, other))
    forward(0)
    note_home(other, m, exps(other, m))
    for j in range(2):
        arrived(outer(j, other), PASSED + j)
        if j == 1:
            arrived(rows.at[pl.ds(6, 2), tail], BOTH)
        m = dots(2 + j, rows.at[j * 4 + 2], rows.at[j * 4 + 3])
        if j == 0:
            forward(1)
        total = exps(2 + j, m)
        note(j, 2, low, m, total)
        note(j, 1, high, m, total)
        tell(j)

    def respond(j):
        arrived(st_in.at[j], STATS + j)
        for slot, place in enumerate((0, 3, 2, 1)):
            mine = st[j, slot, 0:1, :]
            ms = [mine] + [st_in[j, k, slot, 0:1, :] for k in range(3)]
            ts = [st[j, slot, 1:2, :]] + [st_in[j, k, slot, 1:2, :] for k in range(3)]
            top = functools.reduce(jnp.maximum, ms)
            total = sum(t * jnp.exp2((m - top) * SCALE) for m, t in zip(ms, ts, strict=True))
            lane = j * 512 + place * 128
            fac[0:1, lane : lane + 128] = jnp.exp2((mine - top) * SCALE) / total
        for ch, lanes, at, width in ((0, j * 128, 0, 128), (1, j * 128, 128, 128), (2 + j, 0, 256, 256)):
            cols = slice(j * 512 + at, j * 512 + at + width)
            for kt in range(4):
                ks = slice(kt * 256, kt * 256 + 256)
                resp[ks, cols] = (prob[ch, ks, lanes : lanes + width] * fac[0:1, cols]).astype(jnp.bfloat16)

    def along(axis, by, zz=z):
        return dev(y, step(x, by), zz, core) if axis == 0 else dev(step(y, by), x, zz, core)

    place = (x, y)

    class Ring:
        def __init__(self, number):
            self.number, self.axis, self.width = number, number % 2, WIDTHS[number]
            self.at = sum(WIDTHS[:number])
            self.snd1, self.rcv1, self.next, self.part, self.snd2, self.rcv2 = rings[number]
            self.into, self.out = RING + 4 * number, RING_OUT + 2 * number

        def go1(self, kind, ways=(0, 1)):
            for way in ways:
                into = self.into + (kind > 0)
                send(self.snd1.at[kind, way], self.rcv1.at[kind, way], self.out, into, along(self.axis, 1 + 2 * way))

        def dots(self, by, first=0, last=1024):
            dest = step(place[self.axis], by)
            if self.axis == 0:
                parts = [resp[pl.ds(pl.multiple_of(s * 256 + dest * 64, 64), 64), first:last] for s in range(4)]
                left_side = jnp.concatenate(parts, axis=0)
            else:
                left_side = resp[pl.ds(pl.multiple_of(dest * 256, 256), 256), first:last]
            for c in range(0, self.width, 256):
                end = min(c + 256, self.width)
                right = rows[first // 128 : last // 128, :, self.at + c : self.at + end].reshape(last - first, end - c)
                yield slice(c, end), jnp.dot(left_side, right, preferred_element_type=jnp.float32)

        def early(self, ref):
            for cols, v in self.dots(2, 0, 512):
                ref[:, cols] = v

        def far(self, ref=None):
            for cols, v in self.dots(2) if ref is None else self.dots(2, 512, 1024):
                if ref is not None:
                    v = v + ref[:, cols]
                for s in range(4):
                    for way in range(2):
                        self.snd1[0, way, s, :, cols] = v[s * 64 + way * 32 : s * 64 + way * 32 + 32].astype(jnp.bfloat16)

        def beside(self):
            for way in range(2):
                for cols, v in self.dots(1 + 2 * way):
                    for s in range(4):
                        split = [v[s * 64 + half * 32 : s * 64 + half * 32 + 32] for half in range(2)]
                        self.snd1[1, way, s, :, cols] = split[1 - way].astype(jnp.bfloat16)
                        self.next[way, s, :, cols] = split[way]
                self.go1(1, (way,))

        def own(self):
            for cols, v in self.dots(0):
                for s in range(4):
                    for half in range(2):
                        self.part[s, half, :, cols] = v[s * 64 + half * 32 : s * 64 + half * 32 + 32]

        def relay1(self):
            arrived(self.rcv1.at[0], self.into)
            for way in range(2):
                for s in range(4):
                    v = self.next[way, s] + self.rcv1[0, way, s].astype(jnp.float32)
                    self.snd1[2, way, s] = v.astype(jnp.bfloat16)
                self.go1(2, (way,))

        def arrive1(self):
            arrived(self.rcv1.at[pl.ds(1, 2)], self.into + 1)

        def settled(self, by, half):
            s = step(place[1 - self.axis], by)
            passed, plain = self.rcv1[2, half, s], self.rcv1[1, 1 - half, s]
            return self.part[s, half] + passed.astype(jnp.float32) + plain.astype(jnp.float32)

        def go2(self, way, kind):
            into = self.into + 2 + (kind > 0)
            to = along(1 - self.axis, 1 + 2 * way)
            send(self.snd2.at[way, kind], self.rcv2.at[way, kind], self.out + 1, into, to)

        def out2(self):
            for way in range(2):
                self.snd2[way, 0] = encode(self.settled(2, way))
                self.go2(way, 0)

        def beside2(self):
            for way in range(2):
                self.snd2[way, 1] = encode(self.settled(1 + 2 * way, 1 - way))
                self.go2(way, 1)

        def relay2(self):
            values = [self.settled(1 + 2 * way, way) for way in range(2)]
            arrived(self.rcv2.at[pl.ds(0, 2), 0], self.into + 2)
            for way in range(2):
                self.snd2[way, 2] = encode(values[way] + decode(self.rcv2[way, 0]))
                self.go2(way, 2)

        def out_straight(self):
            for across in (1, 0):
                for by in (2, 1, 3, 0):
                    if by or across:
                        slot = 2 * by + across - 1
                        self.snd2[slot] = encode(self.settled(by, zh + across * (1 - 2 * zh)))
                        to = along(1 - self.axis, by, far if across else z)
                        send(self.snd2.at[slot], self.rcv2.at[slot], self.out + 1, self.into + 2, to)

        def end_straight(self):
            mine = self.settled(0, zh)
            arrived(self.rcv2, self.into + 2)
            out_ref[:, self.at : self.at + self.width] = mine + sum(decode(self.rcv2[slot]) for slot in range(7))

        def end2(self):
            fin, zsnd = last[:2]
            cols = slice(self.at, self.at + self.width)
            values = [self.settled(0, half) for half in range(2)]
            arrived(self.rcv2.at[pl.ds(0, 2), pl.ds(1, 2)], self.into + 3)
            for half in range(2):
                fin[half, :, cols] = values[half] + decode(self.rcv2[half, 2]) + decode(self.rcv2[1 - half, 1])
            zsnd[:, cols] = encode(fin[1 - zh, :, cols])

    def out3():
        send(last[1], last[2], FAR_OUT, FAR, dev(y, x, far, core))

    def end3():
        fin, _, zrcv = last
        arrived(zrcv, FAR)
        out_ref[:, : 2 * WIDTHS[0]] = fin[zh] + decode(zrcv[...])

    a0, b0, a1, b1 = (Ring(n) for n in range(4))

    respond(0)
    a0.early(early.at[0])
    b0.early(early.at[1])
    respond(1)
    a0.far(early.at[0])
    a0.go1(0)
    b0.far(early.at[1])
    b0.go1(0)
    for r in (a0, b0):
        r.beside()
    for r in (a0, b0):
        r.own()
    for r in (a1, b1):
        r.far()
    for r in (a0, b0):
        r.relay1()
    for r in (a1, b1):
        r.go1(0)
    for r in (a1, b1):
        r.beside()
        r.own()
    left(rows.at[pl.ds(0, 6)], ROWS_OUT)
    left(st_in, STATS_OUT)
    for r in (a0, b0):
        r.arrive1()
        r.out2()
    for r in (a1, b1):
        r.relay1()
    for r in (a0, b0):
        r.beside2()
    for r in (a0, b0):
        r.relay2()
    for r in (a1, b1):
        r.arrive1()
        r.out_straight()
    for r in (a0, b0):
        r.end2()
    out3()
    for r in (a0, b0, a1, b1):
        left(r.snd1, r.out)
    for r in (a0, b0):
        left(r.snd2, r.out + 1)
    for r in (a1, b1):
        r.end_straight()
    end3()

    total = out_ref[...]
    norm = lax.rsqrt(jnp.sum(total * total, axis=1, keepdims=True) * (1.0 / D) + 1e-06)
    out_ref[...] = total * norm
    for r in (a1, b1):
        left(r.snd2, r.out + 1)
    left(last[1], FAR_OUT)


def ring_buffers(width):
    f32, bf16 = jnp.float32, jnp.bfloat16
    second = pltpu.VMEM((2, 3, 32, width) if width > 256 else (7, 32, width), bf16)
    return [
        pltpu.VMEM((3, 2, 4, 32, width), bf16),
        pltpu.VMEM((3, 2, 4, 32, width), bf16),
        pltpu.VMEM((2, 4, 32, width), f32),
        pltpu.VMEM((4, 2, 32, width), f32),
        second,
        second,
    ]


def per_device(embeddings, centroids):
    f32, bf16 = jnp.float32, jnp.bfloat16
    return pl.pallas_call(
        kernel,
        out_shape=pltpu.VMEM((32, D), f32),
        in_specs=[pl.BlockSpec(memory_space=pl.ANY)] * 2,
        out_specs=pl.BlockSpec(memory_space=pltpu.VMEM),
        scratch_shapes=[
            pltpu.VMEM((KB, D), bf16),
            pltpu.VMEM((8, 128, D), bf16),
            pltpu.VMEM((4, KB, 256), f32),
            pltpu.VMEM((KB, 4 * ROWS), bf16),
            pltpu.VMEM((8, 4 * ROWS), f32),
            pltpu.VMEM((2, 4, 8, 128), f32),
            pltpu.VMEM((2, 3, 4, 8, 128), f32),
            pltpu.VMEM((2, 256, 512), f32),
            [ring_buffers(width) for width in WIDTHS],
            [
                pltpu.VMEM((2, 32, 2 * WIDTHS[0]), f32),
                pltpu.VMEM((32, 2 * WIDTHS[0]), bf16),
                pltpu.VMEM((32, 2 * WIDTHS[0]), bf16),
            ],
            pltpu.SemaphoreType.DMA((3,)),
            pltpu.SemaphoreType.DMA((N_SEND,)),
            pltpu.SemaphoreType.DMA((N_RECEIVE,)),
        ],
        compiler_params=pltpu.CompilerParams(collective_id=0, has_side_effects=True, vmem_limit_bytes=60 * 1024 * 1024),
        cost_estimate=pl.CostEstimate(flops=4 * KB * 4 * ROWS * D, bytes_accessed=5 * 1024 * 1024, transcendentals=KB * KB),
    )(embeddings, centroids)


def solution(mesh):
    placed = (P(("img", "cen"), None), P("cen", None))
    return jax.shard_map(per_device, mesh=mesh, in_specs=placed, out_specs=P(("cen", "img"), None), check_vma=False)
```

```python
import functools
import math

import jax
import jax.numpy as jnp
from jax import lax
from jax.experimental import pallas as pl
from jax.experimental.pallas import tpu as pltpu
from jax.sharding import PartitionSpec as P

MESH = pl.DeviceIdType.MESH
D = 1536
HALF = D // 2
KB = 1024
ROWS = 256
SCALE = D**-0.5 * math.log2(math.e)
SPLIT = (128, 96)
WIDTHS = (512, 512, 256, 256)

HOME = 0
NEAR = 2
PASSED = 4
STATS = 6
RING = 8
BOTH = 24
N_RECEIVE = 25
ROWS_OUT, STATS_OUT, RING_OUT, N_SEND = 0, 1, 2, 10

POWER_SCALE = 2.0**13


def encode(v):
    u = v * POWER_SCALE
    return (u * u * (u * jnp.abs(u))).astype(jnp.bfloat16)


def decode(code):
    c = code.astype(jnp.float32)
    root = lax.rsqrt(lax.rsqrt(jnp.maximum(jnp.abs(c), 2.0**-126))) * (1.0 / POWER_SCALE)
    return jnp.where(c > 0.0, root, jnp.where(c < 0.0, -root, 0.0))


def kernel(e_hbm, c_hbm, out_ref, cen, rows, prob, resp, fac, st, st_in, early, rings, lsem, ssem, rsem):
    img, cpos = lax.axis_index("img"), lax.axis_index("cen")
    y, x, zh = lax.div(img, 8), lax.rem(lax.div(img, 2), 4), lax.rem(img, 2)
    zl, core = lax.div(cpos, 2), lax.rem(cpos, 2)
    z = zh * 2 + zl
    other = 1 - core

    def dev(yy, xx, zz, cc):
        return ((yy * 4 + xx) * 2 + lax.div(zz, 2), lax.rem(zz, 2) * 2 + cc)

    def step(v, by):
        return lax.rem(v + by, 4)

    up, down, far = step(z, 1), step(z, 3), step(z, 2)
    sib = dev(y, x, z, other)
    partners = [dev(y, x, zz, cc) for zz in (up, down) for cc in (0, 1)] + [sib]
    partners += [dev(y, step(x, b), z, core) for b in (1, 3)]
    partners += [dev(step(y, b), x, z, core) for b in (1, 3)]

    def home(j, cc):
        return rows.at[j * 4 + cc]

    def columns(cc):
        return pl.ds(pl.multiple_of(cc * HALF, HALF), HALF)

    def outer(j, cc):
        return rows.at[pl.ds(j * 4 + 2, 2), pl.ds(0, SPLIT[j]), columns(cc)]

    loads = [pltpu.make_async_copy(e_hbm.at[pl.ds(j * 128, 128)], home(j, core), lsem.at[j]) for j in range(2)]
    loads.append(pltpu.make_async_copy(c_hbm, cen, lsem.at[2]))
    for c in loads:
        c.start()

    barrier = pltpu.get_barrier_semaphore()
    for who in partners:
        pl.semaphore_signal(barrier, inc=1, device_id=who, device_id_type=MESH)
    pl.semaphore_wait(barrier, len(partners))

    def copy(src, dst, out, into, who):
        return pltpu.make_async_remote_copy(
            src_ref=src, dst_ref=dst, send_sem=ssem.at[out], recv_sem=rsem.at[into], device_id=who, device_id_type=MESH
        )

    def send(src, dst, out, into, who):
        copy(src, dst, out, into, who).start()

    def arrived(ref, into):
        copy(ref, ref, 0, into, sib).wait_recv()

    def left(ref, out):
        copy(ref, ref, out, 0, sib).wait_send()

    z_to = step(z, 1 + 2 * core)
    for j in range(2):
        for cc in range(2):
            src = e_hbm.at[pl.ds(j * 128, SPLIT[j]), columns(cc)]
            send(src, rows.at[j * 4 + 2 + core, pl.ds(0, SPLIT[j]), columns(cc)], ROWS_OUT, NEAR + j, dev(y, x, z_to, cc))
        send(e_hbm.at[pl.ds(j * 128, 128)], home(j, core), ROWS_OUT, HOME + j, sib)
    tail = pl.ds(SPLIT[1], 128 - SPLIT[1])
    for cc in range(2):
        src = e_hbm.at[pl.ds(128 + SPLIT[1], 128 - SPLIT[1])]
        send(src, rows.at[6 + core, tail], ROWS_OUT, BOTH, dev(y, x, z_to, cc))

    def forward(j):
        arrived(outer(j, core), NEAR + j)
        send(outer(j, core), outer(j, core), ROWS_OUT, PASSED + j, sib)

    def dots(ch, first, second):
        chunk = jnp.concatenate([first[...], second[...]], axis=0)
        m = None
        for kt in range(4):
            s = lax.dot_general(
                cen[kt * 256 : kt * 256 + 256, :],
                chunk,
                (((1,), (1,)), ((), ())),
                preferred_element_type=jnp.float32,
            )
            prob[ch, kt * 256 : kt * 256 + 256, :] = s
            top = jnp.max(s, axis=0, keepdims=True)
            m = top if m is None else jnp.maximum(m, top)
        return m

    def exps(ch, m):
        total = jnp.zeros((1, 256), jnp.float32)
        for kt in range(4):
            e = jnp.exp2((prob[ch, kt * 256 : kt * 256 + 256, :] - m) * SCALE)
            prob[ch, kt * 256 : kt * 256 + 256, :] = e
            total = total + jnp.sum(e, axis=0, keepdims=True)
        return total

    def note(j, slot, lanes, m, total):
        st[j, slot, 0:1, :] = m[:, lanes]
        st[j, slot, 1:2, :] = total[:, lanes]

    low, high = slice(0, 128), slice(128, 256)

    def note_home(ch, m, total):
        for j, lanes in enumerate((low, high)):
            note(j, 3 * ch, lanes, m, total)

    def tell(j):
        for cc in range(2):
            send(st.at[j, pl.ds(0, 2)], st_in.at[j, 1 + core, pl.ds(2, 2)], STATS_OUT, STATS + j, dev(y, x, up, cc))
            send(st.at[j, pl.ds(2, 2)], st_in.at[j, 1 + core, pl.ds(0, 2)], STATS_OUT, STATS + j, dev(y, x, down, cc))
        send(st.at[j], st_in.at[j, 0], STATS_OUT, STATS + j, sib)

    for c in loads:
        c.wait()
    m = dots(core, home(0, core), home(1, core))
    note_home(core, m, exps(core, m))
    for j in range(2):
        arrived(home(j, other), HOME + j)
    m = dots(other, home(0, other), home(1, other))
    forward(0)
    note_home(other, m, exps(other, m))
    for j in range(2):
        arrived(outer(j, other), PASSED + j)
        if j == 1:
            arrived(rows.at[pl.ds(6, 2), tail], BOTH)
        m = dots(2 + j, rows.at[j * 4 + 2], rows.at[j * 4 + 3])
        if j == 0:
            forward(1)
        total = exps(2 + j, m)
        note(j, 2, low, m, total)
        note(j, 1, high, m, total)
        tell(j)

    def respond(j):
        arrived(st_in.at[j], STATS + j)
        for slot, place in enumerate((0, 3, 2, 1)):
            mine = st[j, slot, 0:1, :]
            ms = [mine] + [st_in[j, k, slot, 0:1, :] for k in range(3)]
            ts = [st[j, slot, 1:2, :]] + [st_in[j, k, slot, 1:2, :] for k in range(3)]
            top = functools.reduce(jnp.maximum, ms)
            total = sum(t * jnp.exp2((m - top) * SCALE) for m, t in zip(ms, ts, strict=True))
            lane = j * 512 + place * 128
            fac[0:1, lane : lane + 128] = jnp.exp2((mine - top) * SCALE) / total
        for ch, lanes, at, width in ((0, j * 128, 0, 128), (1, j * 128, 128, 128), (2 + j, 0, 256, 256)):
            cols = slice(j * 512 + at, j * 512 + at + width)
            for kt in range(4):
                ks = slice(kt * 256, kt * 256 + 256)
                resp[ks, cols] = (prob[ch, ks, lanes : lanes + width] * fac[0:1, cols]).astype(jnp.bfloat16)

    def along(axis, by, zz=z):
        return dev(y, step(x, by), zz, core) if axis == 0 else dev(step(y, by), x, zz, core)

    place = (x, y)

    class Ring:
        def __init__(self, number):
            self.number, self.axis, self.width = number, number % 2, WIDTHS[number]
            self.at = sum(WIDTHS[:number])
            self.snd1, self.rcv1, self.next, self.part, self.snd2, self.rcv2 = rings[number]
            self.into, self.out = RING + 4 * number, RING_OUT + 2 * number

        def go1(self, kind, ways=(0, 1)):
            for way in ways:
                into = self.into + (kind > 0)
                send(self.snd1.at[kind, way], self.rcv1.at[kind, way], self.out, into, along(self.axis, 1 + 2 * way))

        def dots(self, by, first=0, last=1024):
            dest = step(place[self.axis], by)
            if self.axis == 0:
                parts = [resp[pl.ds(pl.multiple_of(s * 256 + dest * 64, 64), 64), first:last] for s in range(4)]
                left_side = jnp.concatenate(parts, axis=0)
            else:
                left_side = resp[pl.ds(pl.multiple_of(dest * 256, 256), 256), first:last]
            for c in range(0, self.width, 256):
                end = min(c + 256, self.width)
                right = rows[first // 128 : last // 128, :, self.at + c : self.at + end].reshape(last - first, end - c)
                yield slice(c, end), jnp.dot(left_side, right, preferred_element_type=jnp.float32)

        def early(self, ref):
            for cols, v in self.dots(2, 0, 512):
                ref[:, cols] = v

        def far(self, ref=None):
            for cols, v in self.dots(2) if ref is None else self.dots(2, 512, 1024):
                if ref is not None:
                    v = v + ref[:, cols]
                for s in range(4):
                    for way in range(2):
                        self.snd1[0, way, s, :, cols] = v[s * 64 + way * 32 : s * 64 + way * 32 + 32].astype(jnp.bfloat16)

        def beside(self):
            for way in range(2):
                for cols, v in self.dots(1 + 2 * way):
                    for s in range(4):
                        split = [v[s * 64 + half * 32 : s * 64 + half * 32 + 32] for half in range(2)]
                        self.snd1[1, way, s, :, cols] = split[1 - way].astype(jnp.bfloat16)
                        self.next[way, s, :, cols] = split[way]
                self.go1(1, (way,))

        def own(self):
            for cols, v in self.dots(0):
                for s in range(4):
                    for half in range(2):
                        self.part[s, half, :, cols] = v[s * 64 + half * 32 : s * 64 + half * 32 + 32]

        def relay1(self):
            arrived(self.rcv1.at[0], self.into)
            for way in range(2):
                for s in range(4):
                    v = self.next[way, s] + self.rcv1[0, way, s].astype(jnp.float32)
                    self.snd1[2, way, s] = v.astype(jnp.bfloat16)
                self.go1(2, (way,))

        def arrive1(self):
            arrived(self.rcv1.at[pl.ds(1, 2)], self.into + 1)

        def settled(self, by, half):
            s = step(place[1 - self.axis], by)
            passed, plain = self.rcv1[2, half, s], self.rcv1[1, 1 - half, s]
            return self.part[s, half] + passed.astype(jnp.float32) + plain.astype(jnp.float32)

        def out2(self):
            for way in range(2):
                self.snd2[way] = encode(self.settled(2, way))
                to = along(1 - self.axis, 1 + 2 * way)
                send(self.snd2.at[way], self.rcv2.at[way], self.out + 1, self.into + 2, to)

        def go2(self, way, kind, half):
            across = (half - zh) * (half - zh)
            to = along(1 - self.axis, 1 + 2 * way, step(z, 2 * across))
            src = self.snd2.at[2 * kind + way]
            send(src, self.rcv2.at[2 * kind + across], self.out + 1, self.into + 3, to)

        def beside2(self):
            for way in range(2):
                self.snd2[2 + way] = encode(self.settled(1 + 2 * way, 1 - way))
                self.go2(way, 1, 1 - way)
            self.snd2[6] = encode(self.settled(0, 1 - zh))
            send(self.snd2.at[6], self.rcv2.at[6], self.out + 1, self.into + 3, dev(y, x, far, core))

        def relay2(self):
            values = [self.settled(1 + 2 * way, way) for way in range(2)]
            arrived(self.rcv2.at[pl.ds(0, 2)], self.into + 2)
            for way in range(2):
                self.snd2[4 + way] = encode(values[way] + decode(self.rcv2[way]))
                self.go2(way, 2, way)

        def end2(self):
            mine = self.settled(0, zh)
            arrived(self.rcv2.at[pl.ds(2, 5)], self.into + 3)
            out_ref[:, self.at : self.at + self.width] = mine + sum(decode(self.rcv2[slot]) for slot in range(2, 7))

        def out_straight(self):
            for across in (1, 0):
                for by in (2, 1, 3, 0):
                    if by or across:
                        slot = 2 * by + across - 1
                        self.snd2[slot] = encode(self.settled(by, zh + across * (1 - 2 * zh)))
                        to = along(1 - self.axis, by, far if across else z)
                        send(self.snd2.at[slot], self.rcv2.at[slot], self.out + 1, self.into + 2, to)

        def end_straight(self):
            mine = self.settled(0, zh)
            arrived(self.rcv2, self.into + 2)
            out_ref[:, self.at : self.at + self.width] = mine + sum(decode(self.rcv2[slot]) for slot in range(7))

    a0, b0, a1, b1 = (Ring(n) for n in range(4))

    respond(0)
    a0.early(early.at[0])
    b0.early(early.at[1])
    respond(1)
    a0.far(early.at[0])
    a0.go1(0)
    b0.far(early.at[1])
    b0.go1(0)
    for r in (a0, b0):
        r.beside()
    for r in (a0, b0):
        r.own()
    for r in (a1, b1):
        r.far()
    for r in (a0, b0):
        r.relay1()
    for r in (a1, b1):
        r.go1(0)
    for r in (a1, b1):
        r.beside()
        r.own()
    left(rows.at[pl.ds(0, 6)], ROWS_OUT)
    left(st_in, STATS_OUT)
    for r in (a0, b0):
        r.arrive1()
        r.out2()
    for r in (a1, b1):
        r.relay1()
    for r in (a0, b0):
        r.beside2()
    for r in (a0, b0):
        r.relay2()
    for r in (a1, b1):
        r.arrive1()
        r.out_straight()
    for r in (a0, b0, a1, b1):
        left(r.snd1, r.out)
    for r in (a0, b0):
        left(r.snd2, r.out + 1)
    for r in (a0, b0):
        r.end2()
    for r in (a1, b1):
        r.end_straight()

    total = out_ref[...]
    norm = lax.rsqrt(jnp.sum(total * total, axis=1, keepdims=True) * (1.0 / D) + 1e-06)
    out_ref[...] = total * norm
    for r in (a1, b1):
        left(r.snd2, r.out + 1)


def ring_buffers(width):
    f32, bf16 = jnp.float32, jnp.bfloat16
    second = pltpu.VMEM((7, 32, width), bf16)
    return [
        pltpu.VMEM((3, 2, 4, 32, width), bf16),
        pltpu.VMEM((3, 2, 4, 32, width), bf16),
        pltpu.VMEM((2, 4, 32, width), f32),
        pltpu.VMEM((4, 2, 32, width), f32),
        second,
        second,
    ]


def per_device(embeddings, centroids):
    f32, bf16 = jnp.float32, jnp.bfloat16
    return pl.pallas_call(
        kernel,
        out_shape=pltpu.VMEM((32, D), f32),
        in_specs=[pl.BlockSpec(memory_space=pl.ANY)] * 2,
        out_specs=pl.BlockSpec(memory_space=pltpu.VMEM),
        scratch_shapes=[
            pltpu.VMEM((KB, D), bf16),
            pltpu.VMEM((8, 128, D), bf16),
            pltpu.VMEM((4, KB, 256), f32),
            pltpu.VMEM((KB, 4 * ROWS), bf16),
            pltpu.VMEM((8, 4 * ROWS), f32),
            pltpu.VMEM((2, 4, 8, 128), f32),
            pltpu.VMEM((2, 3, 4, 8, 128), f32),
            pltpu.VMEM((2, 256, 512), f32),
            [ring_buffers(width) for width in WIDTHS],
            pltpu.SemaphoreType.DMA((3,)),
            pltpu.SemaphoreType.DMA((N_SEND,)),
            pltpu.SemaphoreType.DMA((N_RECEIVE,)),
        ],
        compiler_params=pltpu.CompilerParams(collective_id=0, has_side_effects=True, vmem_limit_bytes=60 * 1024 * 1024),
        cost_estimate=pl.CostEstimate(flops=4 * KB * 4 * ROWS * D, bytes_accessed=5 * 1024 * 1024, transcendentals=KB * KB),
    )(embeddings, centroids)


def solution(mesh):
    placed = (P(("img", "cen"), None), P("cen", None))
    return jax.shard_map(per_device, mesh=mesh, in_specs=placed, out_specs=P(("cen", "img"), None), check_vma=False)
```

```python
import functools
import math

import jax
import jax.numpy as jnp
from jax import lax
from jax.experimental import pallas as pl
from jax.experimental.pallas import tpu as pltpu
from jax.sharding import PartitionSpec as P

MESH = pl.DeviceIdType.MESH
D = 1536
HALF = D // 2
KB = 1024
ROWS = 256
SCALE = D**-0.5 * math.log2(math.e)
SPLIT = (128, 96)
WIDTHS = (640, 640, 128, 128)

HOME = 0
NEAR = 2
PASSED = 4
STATS = 6
RING = 8
BOTH = 24
N_RECEIVE = 25
ROWS_OUT, STATS_OUT, RING_OUT, N_SEND = 0, 1, 2, 10

POWER_SCALE = 2.0**13


def encode(v):
    u = v * POWER_SCALE
    return (u * u * (u * jnp.abs(u))).astype(jnp.bfloat16)


def decode(code):
    c = code.astype(jnp.float32)
    root = lax.rsqrt(lax.rsqrt(jnp.maximum(jnp.abs(c), 2.0**-126))) * (1.0 / POWER_SCALE)
    return jnp.where(c > 0.0, root, jnp.where(c < 0.0, -root, 0.0))


def kernel(e_hbm, c_hbm, out_ref, cen, rows, prob, resp, fac, st, st_in, early, rings, lsem, ssem, rsem):
    img, cpos = lax.axis_index("img"), lax.axis_index("cen")
    y, x, zh = lax.div(img, 8), lax.rem(lax.div(img, 2), 4), lax.rem(img, 2)
    zl, core = lax.div(cpos, 2), lax.rem(cpos, 2)
    z = zh * 2 + zl
    other = 1 - core

    def dev(yy, xx, zz, cc):
        return ((yy * 4 + xx) * 2 + lax.div(zz, 2), lax.rem(zz, 2) * 2 + cc)

    def step(v, by):
        return lax.rem(v + by, 4)

    up, down, far = step(z, 1), step(z, 3), step(z, 2)
    sib = dev(y, x, z, other)
    partners = [dev(y, x, zz, cc) for zz in (up, down) for cc in (0, 1)] + [sib]
    partners += [dev(y, step(x, b), z, core) for b in (1, 3)]
    partners += [dev(step(y, b), x, z, core) for b in (1, 3)]

    def home(j, cc):
        return rows.at[j * 4 + cc]

    def columns(cc):
        return pl.ds(pl.multiple_of(cc * HALF, HALF), HALF)

    def outer(j, cc):
        return rows.at[pl.ds(j * 4 + 2, 2), pl.ds(0, SPLIT[j]), columns(cc)]

    loads = [pltpu.make_async_copy(e_hbm.at[pl.ds(j * 128, 128)], home(j, core), lsem.at[j]) for j in range(2)]
    loads.append(pltpu.make_async_copy(c_hbm, cen, lsem.at[2]))
    for c in loads:
        c.start()

    barrier = pltpu.get_barrier_semaphore()
    for who in partners:
        pl.semaphore_signal(barrier, inc=1, device_id=who, device_id_type=MESH)
    pl.semaphore_wait(barrier, len(partners))

    def copy(src, dst, out, into, who):
        return pltpu.make_async_remote_copy(
            src_ref=src, dst_ref=dst, send_sem=ssem.at[out], recv_sem=rsem.at[into], device_id=who, device_id_type=MESH
        )

    def send(src, dst, out, into, who):
        copy(src, dst, out, into, who).start()

    def arrived(ref, into):
        copy(ref, ref, 0, into, sib).wait_recv()

    def left(ref, out):
        copy(ref, ref, out, 0, sib).wait_send()

    z_to = step(z, 1 + 2 * core)
    for j in range(2):
        for cc in range(2):
            src = e_hbm.at[pl.ds(j * 128, SPLIT[j]), columns(cc)]
            send(src, rows.at[j * 4 + 2 + core, pl.ds(0, SPLIT[j]), columns(cc)], ROWS_OUT, NEAR + j, dev(y, x, z_to, cc))
        send(e_hbm.at[pl.ds(j * 128, 128)], home(j, core), ROWS_OUT, HOME + j, sib)
    tail = pl.ds(SPLIT[1], 128 - SPLIT[1])
    for cc in range(2):
        src = e_hbm.at[pl.ds(128 + SPLIT[1], 128 - SPLIT[1])]
        send(src, rows.at[6 + core, tail], ROWS_OUT, BOTH, dev(y, x, z_to, cc))

    def forward(j):
        arrived(outer(j, core), NEAR + j)
        send(outer(j, core), outer(j, core), ROWS_OUT, PASSED + j, sib)

    def dots(ch, first, second):
        chunk = jnp.concatenate([first[...], second[...]], axis=0)
        m = None
        for kt in range(4):
            s = lax.dot_general(
                cen[kt * 256 : kt * 256 + 256, :],
                chunk,
                (((1,), (1,)), ((), ())),
                preferred_element_type=jnp.float32,
            )
            prob[ch, kt * 256 : kt * 256 + 256, :] = s
            top = jnp.max(s, axis=0, keepdims=True)
            m = top if m is None else jnp.maximum(m, top)
        return m

    def exps(ch, m):
        total = jnp.zeros((1, 256), jnp.float32)
        for kt in range(4):
            e = jnp.exp2((prob[ch, kt * 256 : kt * 256 + 256, :] - m) * SCALE)
            prob[ch, kt * 256 : kt * 256 + 256, :] = e
            total = total + jnp.sum(e, axis=0, keepdims=True)
        return total

    def note(j, slot, lanes, m, total):
        st[j, slot, 0:1, :] = m[:, lanes]
        st[j, slot, 1:2, :] = total[:, lanes]

    low, high = slice(0, 128), slice(128, 256)

    def note_home(ch, m, total):
        for j, lanes in enumerate((low, high)):
            note(j, 3 * ch, lanes, m, total)

    def tell(j):
        for cc in range(2):
            send(st.at[j, pl.ds(0, 2)], st_in.at[j, 1 + core, pl.ds(2, 2)], STATS_OUT, STATS + j, dev(y, x, up, cc))
            send(st.at[j, pl.ds(2, 2)], st_in.at[j, 1 + core, pl.ds(0, 2)], STATS_OUT, STATS + j, dev(y, x, down, cc))
        send(st.at[j], st_in.at[j, 0], STATS_OUT, STATS + j, sib)

    for c in loads:
        c.wait()
    m = dots(core, home(0, core), home(1, core))
    note_home(core, m, exps(core, m))
    for j in range(2):
        arrived(home(j, other), HOME + j)
    m = dots(other, home(0, other), home(1, other))
    forward(0)
    note_home(other, m, exps(other, m))
    for j in range(2):
        arrived(outer(j, other), PASSED + j)
        if j == 1:
            arrived(rows.at[pl.ds(6, 2), tail], BOTH)
        m = dots(2 + j, rows.at[j * 4 + 2], rows.at[j * 4 + 3])
        if j == 0:
            forward(1)
        total = exps(2 + j, m)
        note(j, 2, low, m, total)
        note(j, 1, high, m, total)
        tell(j)

    def respond(j):
        arrived(st_in.at[j], STATS + j)
        for slot, place in enumerate((0, 3, 2, 1)):
            mine = st[j, slot, 0:1, :]
            ms = [mine] + [st_in[j, k, slot, 0:1, :] for k in range(3)]
            ts = [st[j, slot, 1:2, :]] + [st_in[j, k, slot, 1:2, :] for k in range(3)]
            top = functools.reduce(jnp.maximum, ms)
            total = sum(t * jnp.exp2((m - top) * SCALE) for m, t in zip(ms, ts, strict=True))
            lane = j * 512 + place * 128
            fac[0:1, lane : lane + 128] = jnp.exp2((mine - top) * SCALE) / total
        for ch, lanes, at, width in ((0, j * 128, 0, 128), (1, j * 128, 128, 128), (2 + j, 0, 256, 256)):
            cols = slice(j * 512 + at, j * 512 + at + width)
            for kt in range(4):
                ks = slice(kt * 256, kt * 256 + 256)
                resp[ks, cols] = (prob[ch, ks, lanes : lanes + width] * fac[0:1, cols]).astype(jnp.bfloat16)

    def along(axis, by, zz=z):
        return dev(y, step(x, by), zz, core) if axis == 0 else dev(step(y, by), x, zz, core)

    place = (x, y)

    class Ring:
        def __init__(self, number):
            self.number, self.axis, self.width = number, number % 2, WIDTHS[number]
            self.at = sum(WIDTHS[:number])
            self.snd1, self.rcv1, self.next, self.part, self.snd2, self.rcv2 = rings[number]
            self.into, self.out = RING + 4 * number, RING_OUT + 2 * number

        def go1(self, kind, ways=(0, 1)):
            for way in ways:
                into = self.into + (kind > 0)
                send(self.snd1.at[kind, way], self.rcv1.at[kind, way], self.out, into, along(self.axis, 1 + 2 * way))

        def dots(self, by, first=0, last=1024):
            dest = step(place[self.axis], by)
            if self.axis == 0:
                parts = [resp[pl.ds(pl.multiple_of(s * 256 + dest * 64, 64), 64), first:last] for s in range(4)]
                left_side = jnp.concatenate(parts, axis=0)
            else:
                left_side = resp[pl.ds(pl.multiple_of(dest * 256, 256), 256), first:last]
            for c in range(0, self.width, 256):
                end = min(c + 256, self.width)
                right = rows[first // 128 : last // 128, :, self.at + c : self.at + end].reshape(last - first, end - c)
                yield slice(c, end), jnp.dot(left_side, right, preferred_element_type=jnp.float32)

        def early(self, ref):
            for cols, v in self.dots(2, 0, 512):
                ref[:, cols] = v

        def far(self, ref=None):
            for cols, v in self.dots(2) if ref is None else self.dots(2, 512, 1024):
                if ref is not None:
                    v = v + ref[:, cols]
                for s in range(4):
                    for way in range(2):
                        self.snd1[0, way, s, :, cols] = v[s * 64 + way * 32 : s * 64 + way * 32 + 32].astype(jnp.bfloat16)

        def beside(self):
            for way in range(2):
                for cols, v in self.dots(1 + 2 * way):
                    for s in range(4):
                        split = [v[s * 64 + half * 32 : s * 64 + half * 32 + 32] for half in range(2)]
                        self.snd1[1, way, s, :, cols] = split[1 - way].astype(jnp.bfloat16)
                        self.next[way, s, :, cols] = split[way]
                self.go1(1, (way,))

        def own(self):
            for cols, v in self.dots(0):
                for s in range(4):
                    for half in range(2):
                        self.part[s, half, :, cols] = v[s * 64 + half * 32 : s * 64 + half * 32 + 32]

        def relay1(self):
            arrived(self.rcv1.at[0], self.into)
            for way in range(2):
                for s in range(4):
                    v = self.next[way, s] + self.rcv1[0, way, s].astype(jnp.float32)
                    self.snd1[2, way, s] = v.astype(jnp.bfloat16)
                self.go1(2, (way,))

        def arrive1(self):
            arrived(self.rcv1.at[pl.ds(1, 2)], self.into + 1)

        def settled(self, by, half):
            s = step(place[1 - self.axis], by)
            passed, plain = self.rcv1[2, half, s], self.rcv1[1, 1 - half, s]
            return self.part[s, half] + passed.astype(jnp.float32) + plain.astype(jnp.float32)

        def out2(self):
            for way in range(2):
                self.snd2[way] = encode(self.settled(2, way))
                to = along(1 - self.axis, 1 + 2 * way)
                send(self.snd2.at[way], self.rcv2.at[way], self.out + 1, self.into + 2, to)

        def go2(self, way, kind, half):
            across = (half - zh) * (half - zh)
            to = along(1 - self.axis, 1 + 2 * way, step(z, 2 * across))
            src = self.snd2.at[2 * kind + way]
            send(src, self.rcv2.at[2 * kind + across], self.out + 1, self.into + 3, to)

        def beside2(self):
            for way in range(2):
                self.snd2[2 + way] = encode(self.settled(1 + 2 * way, 1 - way))
                self.go2(way, 1, 1 - way)
            self.snd2[6] = encode(self.settled(0, 1 - zh))
            send(self.snd2.at[6], self.rcv2.at[6], self.out + 1, self.into + 3, dev(y, x, far, core))

        def relay2(self):
            values = [self.settled(1 + 2 * way, way) for way in range(2)]
            arrived(self.rcv2.at[pl.ds(0, 2)], self.into + 2)
            for way in range(2):
                self.snd2[4 + way] = encode(values[way] + decode(self.rcv2[way]))
                self.go2(way, 2, way)

        def end2(self):
            mine = self.settled(0, zh)
            arrived(self.rcv2.at[pl.ds(2, 5)], self.into + 3)
            out_ref[:, self.at : self.at + self.width] = mine + sum(decode(self.rcv2[slot]) for slot in range(2, 7))

        def out_straight(self):
            for across in (1, 0):
                for by in (2, 1, 3, 0):
                    if by or across:
                        slot = 2 * by + across - 1
                        self.snd2[slot] = encode(self.settled(by, zh + across * (1 - 2 * zh)))
                        to = along(1 - self.axis, by, far if across else z)
                        send(self.snd2.at[slot], self.rcv2.at[slot], self.out + 1, self.into + 2, to)

        def end_straight(self):
            mine = self.settled(0, zh)
            arrived(self.rcv2, self.into + 2)
            out_ref[:, self.at : self.at + self.width] = mine + sum(decode(self.rcv2[slot]) for slot in range(7))

    a0, b0, a1, b1 = (Ring(n) for n in range(4))

    respond(0)
    a0.early(early.at[0])
    b0.early(early.at[1])
    respond(1)
    a0.far(early.at[0])
    a0.go1(0)
    b0.far(early.at[1])
    b0.go1(0)
    for r in (a0, b0):
        r.beside()
    for r in (a0, b0):
        r.own()
    for r in (a1, b1):
        r.far()
    for r in (a0, b0):
        r.relay1()
    for r in (a1, b1):
        r.go1(0)
    for r in (a1, b1):
        r.beside()
        r.own()
    left(rows.at[pl.ds(0, 6)], ROWS_OUT)
    left(st_in, STATS_OUT)
    for r in (a0, b0):
        r.arrive1()
        r.out2()
    for r in (a1, b1):
        r.relay1()
    for r in (a0, b0):
        r.beside2()
    for r in (a0, b0):
        r.relay2()
    for r in (a1, b1):
        r.arrive1()
        r.out_straight()
    for r in (a0, b0, a1, b1):
        left(r.snd1, r.out)
    for r in (a0, b0):
        left(r.snd2, r.out + 1)
    for r in (a0, b0):
        r.end2()
    for r in (a1, b1):
        r.end_straight()

    total = out_ref[...]
    norm = lax.rsqrt(jnp.sum(total * total, axis=1, keepdims=True) * (1.0 / D) + 1e-06)
    out_ref[...] = total * norm
    for r in (a1, b1):
        left(r.snd2, r.out + 1)


def ring_buffers(width):
    f32, bf16 = jnp.float32, jnp.bfloat16
    second = pltpu.VMEM((7, 32, width), bf16)
    return [
        pltpu.VMEM((3, 2, 4, 32, width), bf16),
        pltpu.VMEM((3, 2, 4, 32, width), bf16),
        pltpu.VMEM((2, 4, 32, width), f32),
        pltpu.VMEM((4, 2, 32, width), f32),
        second,
        second,
    ]


def per_device(embeddings, centroids):
    f32, bf16 = jnp.float32, jnp.bfloat16
    return pl.pallas_call(
        kernel,
        out_shape=pltpu.VMEM((32, D), f32),
        in_specs=[pl.BlockSpec(memory_space=pl.ANY)] * 2,
        out_specs=pl.BlockSpec(memory_space=pltpu.VMEM),
        scratch_shapes=[
            pltpu.VMEM((KB, D), bf16),
            pltpu.VMEM((8, 128, D), bf16),
            pltpu.VMEM((4, KB, 256), f32),
            pltpu.VMEM((KB, 4 * ROWS), bf16),
            pltpu.VMEM((8, 4 * ROWS), f32),
            pltpu.VMEM((2, 4, 8, 128), f32),
            pltpu.VMEM((2, 3, 4, 8, 128), f32),
            pltpu.VMEM((2, 256, 640), f32),
            [ring_buffers(width) for width in WIDTHS],
            pltpu.SemaphoreType.DMA((3,)),
            pltpu.SemaphoreType.DMA((N_SEND,)),
            pltpu.SemaphoreType.DMA((N_RECEIVE,)),
        ],
        compiler_params=pltpu.CompilerParams(collective_id=0, has_side_effects=True, vmem_limit_bytes=60 * 1024 * 1024),
        cost_estimate=pl.CostEstimate(flops=4 * KB * 4 * ROWS * D, bytes_accessed=5 * 1024 * 1024, transcendentals=KB * KB),
    )(embeddings, centroids)


def solution(mesh):
    placed = (P(("img", "cen"), None), P("cen", None))
    return jax.shard_map(per_device, mesh=mesh, in_specs=placed, out_specs=P(("cen", "img"), None), check_vma=False)
```

```python
import functools
import math

import jax
import jax.numpy as jnp
from jax import lax
from jax.experimental import pallas as pl
from jax.experimental.pallas import tpu as pltpu
from jax.sharding import PartitionSpec as P

MESH = pl.DeviceIdType.MESH
D = 1536
HALF = D // 2
KB = 1024
ROWS = 256
SCALE = D**-0.5 * math.log2(math.e)
SPLIT = (128, 96)
WIDTHS = (512, 512, 256, 256)

HOME = 0
NEAR = 2
PASSED = 4
STATS = 6
RING = 8
BOTH = 24
N_RECEIVE = 25
ROWS_OUT, STATS_OUT, RING_OUT, N_SEND = 0, 1, 2, 10

POWER_SCALE = 2.0**13


def encode(v):
    u = v * POWER_SCALE
    return (u * u * (u * jnp.abs(u))).astype(jnp.bfloat16)


def decode(code):
    c = code.astype(jnp.float32)
    root = lax.rsqrt(lax.rsqrt(jnp.maximum(jnp.abs(c), 2.0**-126))) * (1.0 / POWER_SCALE)
    return jnp.where(c > 0.0, root, jnp.where(c < 0.0, -root, 0.0))


def kernel(e_hbm, c_hbm, out_ref, cen, rows, prob, resp, fac, st, st_in, early, rings, lsem, ssem, rsem):
    img, cpos = lax.axis_index("img"), lax.axis_index("cen")
    y, x, zh = lax.div(img, 8), lax.rem(lax.div(img, 2), 4), lax.rem(img, 2)
    zl, core = lax.div(cpos, 2), lax.rem(cpos, 2)
    z = zh * 2 + zl
    other = 1 - core

    def dev(yy, xx, zz, cc):
        return ((yy * 4 + xx) * 2 + lax.div(zz, 2), lax.rem(zz, 2) * 2 + cc)

    def step(v, by):
        return lax.rem(v + by, 4)

    up, down, far = step(z, 1), step(z, 3), step(z, 2)
    sib = dev(y, x, z, other)
    partners = [dev(y, x, zz, cc) for zz in (up, down) for cc in (0, 1)] + [sib]
    partners += [dev(y, step(x, b), z, core) for b in (1, 3)]
    partners += [dev(step(y, b), x, z, core) for b in (1, 3)]

    def home(j, cc):
        return rows.at[j * 4 + cc]

    def columns(cc):
        return pl.ds(pl.multiple_of(cc * HALF, HALF), HALF)

    def outer(j, cc):
        return rows.at[pl.ds(j * 4 + 2, 2), pl.ds(0, SPLIT[j]), columns(cc)]

    loads = [pltpu.make_async_copy(e_hbm.at[pl.ds(j * 128, 128)], home(j, core), lsem.at[j]) for j in range(2)]
    loads.append(pltpu.make_async_copy(c_hbm, cen, lsem.at[2]))
    for c in loads:
        c.start()

    barrier = pltpu.get_barrier_semaphore()
    for who in partners:
        pl.semaphore_signal(barrier, inc=1, device_id=who, device_id_type=MESH)
    pl.semaphore_wait(barrier, len(partners))

    def copy(src, dst, out, into, who):
        return pltpu.make_async_remote_copy(
            src_ref=src, dst_ref=dst, send_sem=ssem.at[out], recv_sem=rsem.at[into], device_id=who, device_id_type=MESH
        )

    def send(src, dst, out, into, who):
        copy(src, dst, out, into, who).start()

    def arrived(ref, into):
        copy(ref, ref, 0, into, sib).wait_recv()

    def left(ref, out):
        copy(ref, ref, out, 0, sib).wait_send()

    z_to = step(z, 1 + 2 * core)
    for j in range(2):
        for cc in range(2):
            src = e_hbm.at[pl.ds(j * 128, SPLIT[j]), columns(cc)]
            send(src, rows.at[j * 4 + 2 + core, pl.ds(0, SPLIT[j]), columns(cc)], ROWS_OUT, NEAR + j, dev(y, x, z_to, cc))
        send(e_hbm.at[pl.ds(j * 128, 128)], home(j, core), ROWS_OUT, HOME + j, sib)
    tail = pl.ds(SPLIT[1], 128 - SPLIT[1])
    for cc in range(2):
        src = e_hbm.at[pl.ds(128 + SPLIT[1], 128 - SPLIT[1])]
        send(src, rows.at[6 + core, tail], ROWS_OUT, BOTH, dev(y, x, z_to, cc))

    def forward(j):
        arrived(outer(j, core), NEAR + j)
        send(outer(j, core), outer(j, core), ROWS_OUT, PASSED + j, sib)

    def dots(ch, first, second):
        chunk = jnp.concatenate([first[...], second[...]], axis=0)
        m = None
        for kt in range(4):
            s = lax.dot_general(
                cen[kt * 256 : kt * 256 + 256, :],
                chunk,
                (((1,), (1,)), ((), ())),
                preferred_element_type=jnp.float32,
            )
            prob[ch, kt * 256 : kt * 256 + 256, :] = s
            top = jnp.max(s, axis=0, keepdims=True)
            m = top if m is None else jnp.maximum(m, top)
        return m

    def exps(ch, m):
        total = jnp.zeros((1, 256), jnp.float32)
        for kt in range(4):
            e = jnp.exp2((prob[ch, kt * 256 : kt * 256 + 256, :] - m) * SCALE)
            prob[ch, kt * 256 : kt * 256 + 256, :] = e
            total = total + jnp.sum(e, axis=0, keepdims=True)
        return total

    def note(j, slot, lanes, m, total):
        st[j, slot, 0:1, :] = m[:, lanes]
        st[j, slot, 1:2, :] = total[:, lanes]

    low, high = slice(0, 128), slice(128, 256)

    def note_home(ch, m, total):
        for j, lanes in enumerate((low, high)):
            note(j, 3 * ch, lanes, m, total)

    def tell(j):
        for cc in range(2):
            send(st.at[j, pl.ds(0, 2)], st_in.at[j, 1 + core, pl.ds(2, 2)], STATS_OUT, STATS + j, dev(y, x, up, cc))
            send(st.at[j, pl.ds(2, 2)], st_in.at[j, 1 + core, pl.ds(0, 2)], STATS_OUT, STATS + j, dev(y, x, down, cc))
        send(st.at[j], st_in.at[j, 0], STATS_OUT, STATS + j, sib)

    for c in loads:
        c.wait()
    m = dots(core, home(0, core), home(1, core))
    note_home(core, m, exps(core, m))
    for j in range(2):
        arrived(home(j, other), HOME + j)
    m = dots(other, home(0, other), home(1, other))
    forward(0)
    note_home(other, m, exps(other, m))
    for j in range(2):
        arrived(outer(j, other), PASSED + j)
        if j == 1:
            arrived(rows.at[pl.ds(6, 2), tail], BOTH)
        if j == 0:
            forward(1)
        m = dots(2 + j, rows.at[j * 4 + 2], rows.at[j * 4 + 3])
        total = exps(2 + j, m)
        note(j, 2, low, m, total)
        note(j, 1, high, m, total)
        tell(j)

    def respond(j):
        arrived(st_in.at[j], STATS + j)
        for slot, place in enumerate((0, 3, 2, 1)):
            mine = st[j, slot, 0:1, :]
            ms = [mine] + [st_in[j, k, slot, 0:1, :] for k in range(3)]
            ts = [st[j, slot, 1:2, :]] + [st_in[j, k, slot, 1:2, :] for k in range(3)]
            top = functools.reduce(jnp.maximum, ms)
            total = sum(t * jnp.exp2((m - top) * SCALE) for m, t in zip(ms, ts, strict=True))
            lane = j * 512 + place * 128
            fac[0:1, lane : lane + 128] = jnp.exp2((mine - top) * SCALE) / total
        for ch, lanes, at, width in ((0, j * 128, 0, 128), (1, j * 128, 128, 128), (2 + j, 0, 256, 256)):
            cols = slice(j * 512 + at, j * 512 + at + width)
            for kt in range(4):
                ks = slice(kt * 256, kt * 256 + 256)
                resp[ks, cols] = (prob[ch, ks, lanes : lanes + width] * fac[0:1, cols]).astype(jnp.bfloat16)

    def along(axis, by, zz=z):
        return dev(y, step(x, by), zz, core) if axis == 0 else dev(step(y, by), x, zz, core)

    place = (x, y)

    class Ring:
        def __init__(self, number):
            self.number, self.axis, self.width = number, number % 2, WIDTHS[number]
            self.at = sum(WIDTHS[:number])
            self.snd1, self.rcv1, self.next, self.part, self.snd2, self.rcv2 = rings[number]
            self.into, self.out = RING + 4 * number, RING_OUT + 2 * number

        def go1(self, kind, ways=(0, 1)):
            for way in ways:
                into = self.into + (kind > 0)
                send(self.snd1.at[kind, way], self.rcv1.at[kind, way], self.out, into, along(self.axis, 1 + 2 * way))

        def dots(self, by, first=0, last=1024):
            dest = step(place[self.axis], by)
            if self.axis == 0:
                parts = [resp[pl.ds(pl.multiple_of(s * 256 + dest * 64, 64), 64), first:last] for s in range(4)]
                left_side = jnp.concatenate(parts, axis=0)
            else:
                left_side = resp[pl.ds(pl.multiple_of(dest * 256, 256), 256), first:last]
            for c in range(0, self.width, 256):
                end = min(c + 256, self.width)
                right = rows[first // 128 : last // 128, :, self.at + c : self.at + end].reshape(last - first, end - c)
                yield slice(c, end), jnp.dot(left_side, right, preferred_element_type=jnp.float32)

        def early(self, ref):
            for cols, v in self.dots(2, 0, 512):
                ref[:, cols] = v

        def far(self, ref=None):
            for cols, v in self.dots(2) if ref is None else self.dots(2, 512, 1024):
                if ref is not None:
                    v = v + ref[:, cols]
                for s in range(4):
                    for way in range(2):
                        self.snd1[0, way, s, :, cols] = v[s * 64 + way * 32 : s * 64 + way * 32 + 32].astype(jnp.bfloat16)

        def beside(self):
            for way in range(2):
                for cols, v in self.dots(1 + 2 * way):
                    for s in range(4):
                        split = [v[s * 64 + half * 32 : s * 64 + half * 32 + 32] for half in range(2)]
                        self.snd1[1, way, s, :, cols] = split[1 - way].astype(jnp.bfloat16)
                        self.next[way, s, :, cols] = split[way]
                self.go1(1, (way,))

        def own(self):
            for cols, v in self.dots(0):
                for s in range(4):
                    for half in range(2):
                        self.part[s, half, :, cols] = v[s * 64 + half * 32 : s * 64 + half * 32 + 32]

        def relay1(self):
            arrived(self.rcv1.at[0], self.into)
            for way in range(2):
                for s in range(4):
                    v = self.next[way, s] + self.rcv1[0, way, s].astype(jnp.float32)
                    self.snd1[2, way, s] = v.astype(jnp.bfloat16)
                self.go1(2, (way,))

        def arrive1(self):
            arrived(self.rcv1.at[pl.ds(1, 2)], self.into + 1)

        def settled(self, by, half):
            s = step(place[1 - self.axis], by)
            passed, plain = self.rcv1[2, half, s], self.rcv1[1, 1 - half, s]
            return self.part[s, half] + passed.astype(jnp.float32) + plain.astype(jnp.float32)

        def out2(self):
            for way in range(2):
                self.snd2[way] = encode(self.settled(2, way))
                to = along(1 - self.axis, 1 + 2 * way)
                send(self.snd2.at[way], self.rcv2.at[way], self.out + 1, self.into + 2, to)

        def go2(self, way, kind, half):
            across = (half - zh) * (half - zh)
            to = along(1 - self.axis, 1 + 2 * way, step(z, 2 * across))
            src = self.snd2.at[2 * kind + way]
            send(src, self.rcv2.at[2 * kind + across], self.out + 1, self.into + 3, to)

        def beside2(self):
            for way in range(2):
                self.snd2[2 + way] = encode(self.settled(1 + 2 * way, 1 - way))
                self.go2(way, 1, 1 - way)
            self.snd2[6] = encode(self.settled(0, 1 - zh))
            send(self.snd2.at[6], self.rcv2.at[6], self.out + 1, self.into + 3, dev(y, x, far, core))

        def relay2(self):
            values = [self.settled(1 + 2 * way, way) for way in range(2)]
            arrived(self.rcv2.at[pl.ds(0, 2)], self.into + 2)
            for way in range(2):
                self.snd2[4 + way] = encode(values[way] + decode(self.rcv2[way]))
                self.go2(way, 2, way)

        def end2(self):
            mine = self.settled(0, zh)
            arrived(self.rcv2.at[pl.ds(2, 5)], self.into + 3)
            out_ref[:, self.at : self.at + self.width] = mine + sum(decode(self.rcv2[slot]) for slot in range(2, 7))

        def out_straight(self):
            for across in (1, 0):
                for by in (2, 1, 3, 0):
                    if by or across:
                        slot = 2 * by + across - 1
                        self.snd2[slot] = encode(self.settled(by, zh + across * (1 - 2 * zh)))
                        to = along(1 - self.axis, by, far if across else z)
                        send(self.snd2.at[slot], self.rcv2.at[slot], self.out + 1, self.into + 2, to)

        def end_straight(self):
            mine = self.settled(0, zh)
            arrived(self.rcv2, self.into + 2)
            out_ref[:, self.at : self.at + self.width] = mine + sum(decode(self.rcv2[slot]) for slot in range(7))

    a0, b0, a1, b1 = (Ring(n) for n in range(4))

    respond(0)
    a0.early(early.at[0])
    b0.early(early.at[1])
    respond(1)
    a0.far(early.at[0])
    a0.go1(0)
    b0.far(early.at[1])
    b0.go1(0)
    for r in (a0, b0):
        r.beside()
    for r in (a0, b0):
        r.own()
    for r in (a1, b1):
        r.far()
    for r in (a0, b0):
        r.relay1()
    for r in (a1, b1):
        r.go1(0)
    for r in (a1, b1):
        r.beside()
        r.own()
    left(rows.at[pl.ds(0, 6)], ROWS_OUT)
    left(st_in, STATS_OUT)
    for r in (a0, b0):
        r.arrive1()
        r.out2()
    for r in (a1, b1):
        r.relay1()
    for r in (a0, b0):
        r.beside2()
    for r in (a0, b0):
        r.relay2()
    for r in (a1, b1):
        r.arrive1()
        r.out_straight()
    for r in (a0, b0, a1, b1):
        left(r.snd1, r.out)
    for r in (a0, b0):
        left(r.snd2, r.out + 1)
    for r in (a0, b0):
        r.end2()
    for r in (a1, b1):
        r.end_straight()

    total = out_ref[...]
    norm = lax.rsqrt(jnp.sum(total * total, axis=1, keepdims=True) * (1.0 / D) + 1e-06)
    out_ref[...] = total * norm
    for r in (a1, b1):
        left(r.snd2, r.out + 1)


def ring_buffers(width):
    f32, bf16 = jnp.float32, jnp.bfloat16
    second = pltpu.VMEM((7, 32, width), bf16)
    return [
        pltpu.VMEM((3, 2, 4, 32, width), bf16),
        pltpu.VMEM((3, 2, 4, 32, width), bf16),
        pltpu.VMEM((2, 4, 32, width), f32),
        pltpu.VMEM((4, 2, 32, width), f32),
        second,
        second,
    ]


def per_device(embeddings, centroids):
    f32, bf16 = jnp.float32, jnp.bfloat16
    return pl.pallas_call(
        kernel,
        out_shape=pltpu.VMEM((32, D), f32),
        in_specs=[pl.BlockSpec(memory_space=pl.ANY)] * 2,
        out_specs=pl.BlockSpec(memory_space=pltpu.VMEM),
        scratch_shapes=[
            pltpu.VMEM((KB, D), bf16),
            pltpu.VMEM((8, 128, D), bf16),
            pltpu.VMEM((4, KB, 256), f32),
            pltpu.VMEM((KB, 4 * ROWS), bf16),
            pltpu.VMEM((8, 4 * ROWS), f32),
            pltpu.VMEM((2, 4, 8, 128), f32),
            pltpu.VMEM((2, 3, 4, 8, 128), f32),
            pltpu.VMEM((2, 256, 512), f32),
            [ring_buffers(width) for width in WIDTHS],
            pltpu.SemaphoreType.DMA((3,)),
            pltpu.SemaphoreType.DMA((N_SEND,)),
            pltpu.SemaphoreType.DMA((N_RECEIVE,)),
        ],
        compiler_params=pltpu.CompilerParams(collective_id=0, has_side_effects=True, vmem_limit_bytes=60 * 1024 * 1024),
        cost_estimate=pl.CostEstimate(flops=4 * KB * 4 * ROWS * D, bytes_accessed=5 * 1024 * 1024, transcendentals=KB * KB),
    )(embeddings, centroids)


def solution(mesh):
    placed = (P(("img", "cen"), None), P("cen", None))
    return jax.shard_map(per_device, mesh=mesh, in_specs=placed, out_specs=P(("cen", "img"), None), check_vma=False)
```

```python
import functools
import math

import jax
import jax.numpy as jnp
from jax import lax
from jax.experimental import pallas as pl
from jax.experimental.pallas import tpu as pltpu
from jax.sharding import PartitionSpec as P

MESH = pl.DeviceIdType.MESH
D = 1536
HALF = D // 2
KB = 1024
ROWS = 256
SCALE = D**-0.5 * math.log2(math.e)
SPLIT = (128, 96)
WIDTHS = (512, 512, 256, 256)

HOME = 0
NEAR = 2
PASSED = 4
STATS = 6
RING = 8
BOTH = 24
N_RECEIVE = 25
ROWS_OUT, STATS_OUT, RING_OUT, N_SEND = 0, 1, 2, 10

POWER_SCALE = 2.0**13


def encode(v):
    u = v * POWER_SCALE
    return (u * u * (u * jnp.abs(u))).astype(jnp.bfloat16)


def decode(code):
    c = code.astype(jnp.float32)
    root = lax.rsqrt(lax.rsqrt(jnp.maximum(jnp.abs(c), 2.0**-126))) * (1.0 / POWER_SCALE)
    return jnp.where(c > 0.0, root, jnp.where(c < 0.0, -root, 0.0))


def kernel(e_hbm, c_hbm, out_ref, cen, rows, prob, resp, fac, st, st_in, early, rings, lsem, ssem, rsem):
    img, cpos = lax.axis_index("img"), lax.axis_index("cen")
    y, x, zh = lax.div(img, 8), lax.rem(lax.div(img, 2), 4), lax.rem(img, 2)
    zl, core = lax.div(cpos, 2), lax.rem(cpos, 2)
    z = zh * 2 + zl
    other = 1 - core

    def dev(yy, xx, zz, cc):
        return ((yy * 4 + xx) * 2 + lax.div(zz, 2), lax.rem(zz, 2) * 2 + cc)

    def step(v, by):
        return lax.rem(v + by, 4)

    up, down, far = step(z, 1), step(z, 3), step(z, 2)
    sib = dev(y, x, z, other)
    partners = [dev(y, x, down, 0), dev(y, x, up, 1), sib]
    partners += [dev(y, step(x, b), z, core) for b in (1, 3)]
    partners += [dev(step(y, b), x, z, core) for b in (1, 3)]

    def home(j, cc):
        return rows.at[j * 4 + cc]

    def columns(cc):
        return pl.ds(pl.multiple_of(cc * HALF, HALF), HALF)

    def outer(j, cc):
        return rows.at[pl.ds(j * 4 + 2, 2), pl.ds(0, SPLIT[j]), columns(cc)]

    loads = [pltpu.make_async_copy(e_hbm.at[pl.ds(j * 128, 128)], home(j, core), lsem.at[j]) for j in range(2)]
    loads.append(pltpu.make_async_copy(c_hbm, cen, lsem.at[2]))
    for c in loads:
        c.start()

    barrier = pltpu.get_barrier_semaphore()
    for who in partners:
        pl.semaphore_signal(barrier, inc=1, device_id=who, device_id_type=MESH)
    pl.semaphore_wait(barrier, len(partners))

    def copy(src, dst, out, into, who):
        return pltpu.make_async_remote_copy(
            src_ref=src, dst_ref=dst, send_sem=ssem.at[out], recv_sem=rsem.at[into], device_id=who, device_id_type=MESH
        )

    def send(src, dst, out, into, who):
        copy(src, dst, out, into, who).start()

    def arrived(ref, into):
        copy(ref, ref, 0, into, sib).wait_recv()

    def left(ref, out):
        copy(ref, ref, out, 0, sib).wait_send()

    z_to = step(z, 1 + 2 * core)
    for j in range(2):
        for cc in range(2):
            src = e_hbm.at[pl.ds(j * 128, SPLIT[j]), columns(cc)]
            send(src, rows.at[j * 4 + 2 + core, pl.ds(0, SPLIT[j]), columns(cc)], ROWS_OUT, NEAR + j, dev(y, x, z_to, cc))
        send(e_hbm.at[pl.ds(j * 128, 128)], home(j, core), ROWS_OUT, HOME + j, sib)
    tail = pl.ds(SPLIT[1], 128 - SPLIT[1])
    for cc in range(2):
        src = e_hbm.at[pl.ds(128 + SPLIT[1], 128 - SPLIT[1])]
        send(src, rows.at[6 + core, tail], ROWS_OUT, BOTH, dev(y, x, z_to, cc))

    def forward(j):
        arrived(outer(j, core), NEAR + j)
        send(outer(j, core), outer(j, core), ROWS_OUT, PASSED + j, sib)

    def dots(ch, first, second):
        chunk = jnp.concatenate([first[...], second[...]], axis=0)
        m = None
        for kt in range(4):
            s = lax.dot_general(
                cen[kt * 256 : kt * 256 + 256, :],
                chunk,
                (((1,), (1,)), ((), ())),
                preferred_element_type=jnp.float32,
            )
            prob[ch, kt * 256 : kt * 256 + 256, :] = s
            top = jnp.max(s, axis=0, keepdims=True)
            m = top if m is None else jnp.maximum(m, top)
        return m

    def exps(ch, m):
        total = jnp.zeros((1, 256), jnp.float32)
        for kt in range(4):
            e = jnp.exp2((prob[ch, kt * 256 : kt * 256 + 256, :] - m) * SCALE)
            prob[ch, kt * 256 : kt * 256 + 256, :] = e
            total = total + jnp.sum(e, axis=0, keepdims=True)
        return total

    def note(j, slot, lanes, m, total):
        st[j, slot, 0:1, :] = m[:, lanes]
        st[j, slot, 1:2, :] = total[:, lanes]

    low, high = slice(0, 128), slice(128, 256)

    def note_home(ch, m, total):
        for j, lanes in enumerate((low, high)):
            note(j, 3 * ch, lanes, m, total)

    def tell(j):
        for cc in range(2):
            send(st.at[j, pl.ds(0, 2)], st_in.at[j, 1 + core, pl.ds(2, 2)], STATS_OUT, STATS + j, dev(y, x, up, cc))
            send(st.at[j, pl.ds(2, 2)], st_in.at[j, 1 + core, pl.ds(0, 2)], STATS_OUT, STATS + j, dev(y, x, down, cc))
        send(st.at[j], st_in.at[j, 0], STATS_OUT, STATS + j, sib)

    for c in loads:
        c.wait()
    m = dots(core, home(0, core), home(1, core))
    note_home(core, m, exps(core, m))
    for j in range(2):
        arrived(home(j, other), HOME + j)
    m = dots(other, home(0, other), home(1, other))
    forward(0)
    note_home(other, m, exps(other, m))
    for j in range(2):
        arrived(outer(j, other), PASSED + j)
        if j == 1:
            arrived(rows.at[pl.ds(6, 2), tail], BOTH)
        if j == 0:
            forward(1)
        m = dots(2 + j, rows.at[j * 4 + 2], rows.at[j * 4 + 3])
        total = exps(2 + j, m)
        note(j, 2, low, m, total)
        note(j, 1, high, m, total)
        tell(j)

    def respond(j):
        arrived(st_in.at[j], STATS + j)
        for slot, place in enumerate((0, 3, 2, 1)):
            mine = st[j, slot, 0:1, :]
            ms = [mine] + [st_in[j, k, slot, 0:1, :] for k in range(3)]
            ts = [st[j, slot, 1:2, :]] + [st_in[j, k, slot, 1:2, :] for k in range(3)]
            top = functools.reduce(jnp.maximum, ms)
            total = sum(t * jnp.exp2((m - top) * SCALE) for m, t in zip(ms, ts, strict=True))
            lane = j * 512 + place * 128
            fac[0:1, lane : lane + 128] = jnp.exp2((mine - top) * SCALE) / total
        for ch, lanes, at, width in ((0, j * 128, 0, 128), (1, j * 128, 128, 128), (2 + j, 0, 256, 256)):
            cols = slice(j * 512 + at, j * 512 + at + width)
            for kt in range(4):
                ks = slice(kt * 256, kt * 256 + 256)
                resp[ks, cols] = (prob[ch, ks, lanes : lanes + width] * fac[0:1, cols]).astype(jnp.bfloat16)

    def along(axis, by, zz=z):
        return dev(y, step(x, by), zz, core) if axis == 0 else dev(step(y, by), x, zz, core)

    place = (x, y)

    class Ring:
        def __init__(self, number):
            self.number, self.axis, self.width = number, number % 2, WIDTHS[number]
            self.at = sum(WIDTHS[:number])
            self.snd1, self.rcv1, self.next, self.part, self.snd2, self.rcv2 = rings[number]
            self.into, self.out = RING + 4 * number, RING_OUT + 2 * number

        def go1(self, kind, ways=(0, 1)):
            for way in ways:
                into = self.into + (kind > 0)
                send(self.snd1.at[kind, way], self.rcv1.at[kind, way], self.out, into, along(self.axis, 1 + 2 * way))

        def dots(self, by, first=0, last=1024):
            dest = step(place[self.axis], by)
            if self.axis == 0:
                parts = [resp[pl.ds(pl.multiple_of(s * 256 + dest * 64, 64), 64), first:last] for s in range(4)]
                left_side = jnp.concatenate(parts, axis=0)
            else:
                left_side = resp[pl.ds(pl.multiple_of(dest * 256, 256), 256), first:last]
            for c in range(0, self.width, 256):
                end = min(c + 256, self.width)
                right = rows[first // 128 : last // 128, :, self.at + c : self.at + end].reshape(last - first, end - c)
                yield slice(c, end), jnp.dot(left_side, right, preferred_element_type=jnp.float32)

        def early(self, ref):
            for cols, v in self.dots(2, 0, 512):
                ref[:, cols] = v

        def far(self, ref=None):
            for cols, v in self.dots(2) if ref is None else self.dots(2, 512, 1024):
                if ref is not None:
                    v = v + ref[:, cols]
                for s in range(4):
                    for way in range(2):
                        self.snd1[0, way, s, :, cols] = v[s * 64 + way * 32 : s * 64 + way * 32 + 32].astype(jnp.bfloat16)

        def beside(self):
            for way in range(2):
                for cols, v in self.dots(1 + 2 * way):
                    for s in range(4):
                        split = [v[s * 64 + half * 32 : s * 64 + half * 32 + 32] for half in range(2)]
                        self.snd1[1, way, s, :, cols] = split[1 - way].astype(jnp.bfloat16)
                        self.next[way, s, :, cols] = split[way]
                self.go1(1, (way,))

        def own(self):
            for cols, v in self.dots(0):
                for s in range(4):
                    for half in range(2):
                        self.part[s, half, :, cols] = v[s * 64 + half * 32 : s * 64 + half * 32 + 32]

        def relay1(self):
            arrived(self.rcv1.at[0], self.into)
            for way in range(2):
                for s in range(4):
                    v = self.next[way, s] + self.rcv1[0, way, s].astype(jnp.float32)
                    self.snd1[2, way, s] = v.astype(jnp.bfloat16)
                self.go1(2, (way,))

        def arrive1(self):
            arrived(self.rcv1.at[pl.ds(1, 2)], self.into + 1)

        def settled(self, by, half):
            s = step(place[1 - self.axis], by)
            passed, plain = self.rcv1[2, half, s], self.rcv1[1, 1 - half, s]
            return self.part[s, half] + passed.astype(jnp.float32) + plain.astype(jnp.float32)

        def out2(self):
            for way in range(2):
                self.snd2[way] = encode(self.settled(2, way))
                to = along(1 - self.axis, 1 + 2 * way)
                send(self.snd2.at[way], self.rcv2.at[way], self.out + 1, self.into + 2, to)

        def go2(self, way, kind, half):
            across = (half - zh) * (half - zh)
            to = along(1 - self.axis, 1 + 2 * way, step(z, 2 * across))
            src = self.snd2.at[2 * kind + way]
            send(src, self.rcv2.at[2 * kind + across], self.out + 1, self.into + 3, to)

        def beside2(self):
            for way in range(2):
                self.snd2[2 + way] = encode(self.settled(1 + 2 * way, 1 - way))
                self.go2(way, 1, 1 - way)
            self.snd2[6] = encode(self.settled(0, 1 - zh))
            send(self.snd2.at[6], self.rcv2.at[6], self.out + 1, self.into + 3, dev(y, x, far, core))

        def relay2(self):
            values = [self.settled(1 + 2 * way, way) for way in range(2)]
            arrived(self.rcv2.at[pl.ds(0, 2)], self.into + 2)
            for way in range(2):
                self.snd2[4 + way] = encode(values[way] + decode(self.rcv2[way]))
                self.go2(way, 2, way)

        def end2(self):
            mine = self.settled(0, zh)
            arrived(self.rcv2.at[pl.ds(2, 5)], self.into + 3)
            out_ref[:, self.at : self.at + self.width] = mine + sum(decode(self.rcv2[slot]) for slot in range(2, 7))

        def out_straight(self):
            for across in (1, 0):
                for by in (2, 1, 3, 0):
                    if by or across:
                        slot = 2 * by + across - 1
                        self.snd2[slot] = encode(self.settled(by, zh + across * (1 - 2 * zh)))
                        to = along(1 - self.axis, by, far if across else z)
                        send(self.snd2.at[slot], self.rcv2.at[slot], self.out + 1, self.into + 2, to)

        def end_straight(self):
            mine = self.settled(0, zh)
            arrived(self.rcv2, self.into + 2)
            out_ref[:, self.at : self.at + self.width] = mine + sum(decode(self.rcv2[slot]) for slot in range(7))

    a0, b0, a1, b1 = (Ring(n) for n in range(4))

    respond(0)
    a0.early(early.at[0])
    b0.early(early.at[1])
    respond(1)
    a0.far(early.at[0])
    a0.go1(0)
    b0.far(early.at[1])
    b0.go1(0)
    for r in (a0, b0):
        r.beside()
    for r in (a0, b0):
        r.own()
    for r in (a1, b1):
        r.far()
    for r in (a0, b0):
        r.relay1()
    for r in (a1, b1):
        r.go1(0)
    for r in (a1, b1):
        r.beside()
        r.own()
    left(rows.at[pl.ds(0, 6)], ROWS_OUT)
    left(st_in, STATS_OUT)
    for r in (a0, b0):
        r.arrive1()
        r.out2()
    for r in (a1, b1):
        r.relay1()
    for r in (a0, b0):
        r.beside2()
    for r in (a0, b0):
        r.relay2()
    for r in (a1, b1):
        r.arrive1()
        r.out_straight()
    for r in (a0, b0, a1, b1):
        left(r.snd1, r.out)
    for r in (a0, b0):
        left(r.snd2, r.out + 1)
    for r in (a0, b0):
        r.end2()
    for r in (a1, b1):
        r.end_straight()

    total = out_ref[...]
    norm = lax.rsqrt(jnp.sum(total * total, axis=1, keepdims=True) * (1.0 / D) + 1e-06)
    out_ref[...] = total * norm
    for r in (a1, b1):
        left(r.snd2, r.out + 1)


def ring_buffers(width):
    f32, bf16 = jnp.float32, jnp.bfloat16
    second = pltpu.VMEM((7, 32, width), bf16)
    return [
        pltpu.VMEM((3, 2, 4, 32, width), bf16),
        pltpu.VMEM((3, 2, 4, 32, width), bf16),
        pltpu.VMEM((2, 4, 32, width), f32),
        pltpu.VMEM((4, 2, 32, width), f32),
        second,
        second,
    ]


def per_device(embeddings, centroids):
    f32, bf16 = jnp.float32, jnp.bfloat16
    return pl.pallas_call(
        kernel,
        out_shape=pltpu.VMEM((32, D), f32),
        in_specs=[pl.BlockSpec(memory_space=pl.ANY)] * 2,
        out_specs=pl.BlockSpec(memory_space=pltpu.VMEM),
        scratch_shapes=[
            pltpu.VMEM((KB, D), bf16),
            pltpu.VMEM((8, 128, D), bf16),
            pltpu.VMEM((4, KB, 256), f32),
            pltpu.VMEM((KB, 4 * ROWS), bf16),
            pltpu.VMEM((8, 4 * ROWS), f32),
            pltpu.VMEM((2, 4, 8, 128), f32),
            pltpu.VMEM((2, 3, 4, 8, 128), f32),
            pltpu.VMEM((2, 256, 512), f32),
            [ring_buffers(width) for width in WIDTHS],
            pltpu.SemaphoreType.DMA((3,)),
            pltpu.SemaphoreType.DMA((N_SEND,)),
            pltpu.SemaphoreType.DMA((N_RECEIVE,)),
        ],
        compiler_params=pltpu.CompilerParams(collective_id=0, has_side_effects=True, vmem_limit_bytes=60 * 1024 * 1024),
        cost_estimate=pl.CostEstimate(flops=4 * KB * 4 * ROWS * D, bytes_accessed=5 * 1024 * 1024, transcendentals=KB * KB),
    )(embeddings, centroids)


def solution(mesh):
    placed = (P(("img", "cen"), None), P("cen", None))
    return jax.shard_map(per_device, mesh=mesh, in_specs=placed, out_specs=P(("cen", "img"), None), check_vma=False)
```

```python
import functools
import math

import jax
import jax.numpy as jnp
from jax import lax
from jax.experimental import pallas as pl
from jax.experimental.pallas import tpu as pltpu
from jax.sharding import PartitionSpec as P

MESH = pl.DeviceIdType.MESH
D = 1536
HALF = D // 2
KB = 1024
ROWS = 256
SCALE = D**-0.5 * math.log2(math.e)
SPLIT = (128, 96)
WIDTHS = (512, 512, 256, 256)

HOME = 0
NEAR = 2
PASSED = 4
STATS = 6
RING = 8
BOTH = 24
N_RECEIVE = 25
ROWS_OUT, STATS_OUT, RING_OUT, N_SEND = 0, 1, 2, 10

POWER_SCALE = 2.0**13


def encode(v):
    u = v * POWER_SCALE
    return (u * u * (u * jnp.abs(u))).astype(jnp.bfloat16)


def decode(code):
    c = code.astype(jnp.float32)
    root = lax.rsqrt(lax.rsqrt(jnp.maximum(jnp.abs(c), 2.0**-126))) * (1.0 / POWER_SCALE)
    return jnp.where(c > 0.0, root, jnp.where(c < 0.0, -root, 0.0))


def kernel(e_hbm, c_hbm, out_ref, cen, rows, prob, resp, fac, st, st_in, early, rings, lsem, ssem, rsem):
    img, cpos = lax.axis_index("img"), lax.axis_index("cen")
    y, x, zh = lax.div(img, 8), lax.rem(lax.div(img, 2), 4), lax.rem(img, 2)
    zl, core = lax.div(cpos, 2), lax.rem(cpos, 2)
    z = zh * 2 + zl
    other = 1 - core

    def dev(yy, xx, zz, cc):
        return ((yy * 4 + xx) * 2 + lax.div(zz, 2), lax.rem(zz, 2) * 2 + cc)

    def step(v, by):
        return lax.rem(v + by, 4)

    up, down, far = step(z, 1), step(z, 3), step(z, 2)
    sib = dev(y, x, z, other)
    partners = [dev(y, x, down, 0), dev(y, x, up, 1), sib]
    partners += [dev(y, step(x, b), z, core) for b in (1, 3)]
    partners += [dev(step(y, b), x, z, core) for b in (1, 3)]

    def home(j, cc):
        return rows.at[j * 4 + cc]

    def columns(cc):
        return pl.ds(pl.multiple_of(cc * HALF, HALF), HALF)

    def outer(j, cc):
        return rows.at[pl.ds(j * 4 + 2, 2), pl.ds(0, SPLIT[j]), columns(cc)]

    loads = [pltpu.make_async_copy(e_hbm.at[pl.ds(j * 128, 128)], home(j, core), lsem.at[j]) for j in range(2)]
    loads.append(pltpu.make_async_copy(c_hbm, cen, lsem.at[2]))
    for c in loads:
        c.start()

    barrier = pltpu.get_barrier_semaphore()
    for who in partners:
        pl.semaphore_signal(barrier, inc=1, device_id=who, device_id_type=MESH)
    pl.semaphore_wait(barrier, len(partners))

    def copy(src, dst, out, into, who):
        return pltpu.make_async_remote_copy(
            src_ref=src, dst_ref=dst, send_sem=ssem.at[out], recv_sem=rsem.at[into], device_id=who, device_id_type=MESH
        )

    def send(src, dst, out, into, who):
        copy(src, dst, out, into, who).start()

    def arrived(ref, into):
        copy(ref, ref, 0, into, sib).wait_recv()

    def left(ref, out):
        copy(ref, ref, out, 0, sib).wait_send()

    z_to = step(z, 1 + 2 * core)
    for j in range(2):
        for cc in range(2):
            src = e_hbm.at[pl.ds(j * 128, SPLIT[j]), columns(cc)]
            send(src, rows.at[j * 4 + 2 + core, pl.ds(0, SPLIT[j]), columns(cc)], ROWS_OUT, NEAR + j, dev(y, x, z_to, cc))
        send(e_hbm.at[pl.ds(j * 128, 128)], home(j, core), ROWS_OUT, HOME + j, sib)
    tail = pl.ds(SPLIT[1], 128 - SPLIT[1])
    for cc in range(2):
        src = e_hbm.at[pl.ds(128 + SPLIT[1], 128 - SPLIT[1])]
        send(src, rows.at[6 + core, tail], ROWS_OUT, BOTH, dev(y, x, z_to, cc))

    def forward(j):
        arrived(outer(j, core), NEAR + j)
        send(outer(j, core), outer(j, core), ROWS_OUT, PASSED + j, sib)

    def dots(ch, first, second):
        chunk = jnp.concatenate([first[...], second[...]], axis=0)
        m = None
        for kt in range(4):
            s = lax.dot_general(
                cen[kt * 256 : kt * 256 + 256, :],
                chunk,
                (((1,), (1,)), ((), ())),
                preferred_element_type=jnp.float32,
            )
            prob[ch, kt * 256 : kt * 256 + 256, :] = s
            top = jnp.max(s, axis=0, keepdims=True)
            m = top if m is None else jnp.maximum(m, top)
        return m

    def exps(ch, m):
        total = jnp.zeros((1, 256), jnp.float32)
        for kt in range(4):
            e = jnp.exp2((prob[ch, kt * 256 : kt * 256 + 256, :] - m) * SCALE)
            prob[ch, kt * 256 : kt * 256 + 256, :] = e
            total = total + jnp.sum(e, axis=0, keepdims=True)
        return total

    def note(j, slot, lanes, m, total):
        st[j, slot, 0:1, :] = m[:, lanes]
        st[j, slot, 1:2, :] = total[:, lanes]

    low, high = slice(0, 128), slice(128, 256)

    def note_home(ch, m, total):
        for j, lanes in enumerate((low, high)):
            note(j, 3 * ch, lanes, m, total)

    def tell(j):
        for cc in range(2):
            send(st.at[j, pl.ds(0, 2)], st_in.at[j, 1 + core, pl.ds(2, 2)], STATS_OUT, STATS + j, dev(y, x, up, cc))
            send(st.at[j, pl.ds(2, 2)], st_in.at[j, 1 + core, pl.ds(0, 2)], STATS_OUT, STATS + j, dev(y, x, down, cc))
        send(st.at[j], st_in.at[j, 0], STATS_OUT, STATS + j, sib)

    for c in loads:
        c.wait()
    m = dots(core, home(0, core), home(1, core))
    note_home(core, m, exps(core, m))
    for j in range(2):
        arrived(home(j, other), HOME + j)
    m = dots(other, home(0, other), home(1, other))
    forward(0)
    note_home(other, m, exps(other, m))
    for j in range(2):
        arrived(outer(j, other), PASSED + j)
        if j == 1:
            arrived(rows.at[pl.ds(6, 2), tail], BOTH)
        if j == 0:
            forward(1)
        m = dots(2 + j, rows.at[j * 4 + 2], rows.at[j * 4 + 3])
        total = exps(2 + j, m)
        note(j, 2, low, m, total)
        note(j, 1, high, m, total)
        tell(j)

    def respond(j):
        arrived(st_in.at[j], STATS + j)
        for slot, place in enumerate((0, 3, 2, 1)):
            mine = st[j, slot, 0:1, :]
            ms = [mine] + [st_in[j, k, slot, 0:1, :] for k in range(3)]
            ts = [st[j, slot, 1:2, :]] + [st_in[j, k, slot, 1:2, :] for k in range(3)]
            top = functools.reduce(jnp.maximum, ms)
            total = sum(t * jnp.exp2((m - top) * SCALE) for m, t in zip(ms, ts, strict=True))
            lane = j * 512 + place * 128
            fac[0:1, lane : lane + 128] = jnp.exp2((mine - top) * SCALE) / total
        for ch, lanes, at, width in ((0, j * 128, 0, 128), (1, j * 128, 128, 128), (2 + j, 0, 256, 256)):
            cols = slice(j * 512 + at, j * 512 + at + width)
            for kt in range(4):
                ks = slice(kt * 256, kt * 256 + 256)
                resp[ks, cols] = (prob[ch, ks, lanes : lanes + width] * fac[0:1, cols]).astype(jnp.bfloat16)

    def along(axis, by, zz=z):
        return dev(y, step(x, by), zz, core) if axis == 0 else dev(step(y, by), x, zz, core)

    place = (x, y)

    class Ring:
        def __init__(self, number):
            self.number, self.axis, self.width = number, number % 2, WIDTHS[number]
            self.at = sum(WIDTHS[:number])
            self.snd1, self.rcv1, self.next, self.part, self.snd2, self.rcv2 = rings[number]
            self.into, self.out = RING + 4 * number, RING_OUT + 2 * number

        def go1(self, kind, ways=(0, 1)):
            for way in ways:
                into = self.into + (kind > 0)
                send(self.snd1.at[kind, way], self.rcv1.at[kind, way], self.out, into, along(self.axis, 1 + 2 * way))

        def dots(self, by, first=0, last=1024):
            dest = step(place[self.axis], by)
            if self.axis == 0:
                parts = [resp[pl.ds(pl.multiple_of(s * 256 + dest * 64, 64), 64), first:last] for s in range(4)]
                left_side = jnp.concatenate(parts, axis=0)
            else:
                left_side = resp[pl.ds(pl.multiple_of(dest * 256, 256), 256), first:last]
            for c in range(0, self.width, 256):
                end = min(c + 256, self.width)
                right = rows[first // 128 : last // 128, :, self.at + c : self.at + end].reshape(last - first, end - c)
                yield slice(c, end), jnp.dot(left_side, right, preferred_element_type=jnp.float32)

        def early(self, ref):
            for cols, v in self.dots(2, 0, 512):
                ref[:, cols] = v

        def far(self, ref=None):
            for cols, v in self.dots(2) if ref is None else self.dots(2, 512, 1024):
                if ref is not None:
                    v = v + ref[:, cols]
                for s in range(4):
                    for way in range(2):
                        self.snd1[0, way, s, :, cols] = v[s * 64 + way * 32 : s * 64 + way * 32 + 32].astype(jnp.bfloat16)

        def beside(self):
            for way in range(2):
                for cols, v in self.dots(1 + 2 * way):
                    for s in range(4):
                        split = [v[s * 64 + half * 32 : s * 64 + half * 32 + 32] for half in range(2)]
                        self.snd1[1, way, s, :, cols] = split[1 - way].astype(jnp.bfloat16)
                        self.next[way, s, :, cols] = split[way]
                self.go1(1, (way,))

        def own(self):
            for cols, v in self.dots(0):
                for s in range(4):
                    for half in range(2):
                        self.part[s, half, :, cols] = v[s * 64 + half * 32 : s * 64 + half * 32 + 32]

        def relay1(self):
            arrived(self.rcv1.at[0], self.into)
            for way in range(2):
                for s in range(4):
                    v = self.next[way, s] + self.rcv1[0, way, s].astype(jnp.float32)
                    self.snd1[2, way, s] = v.astype(jnp.bfloat16)
                self.go1(2, (way,))

        def arrive1(self):
            arrived(self.rcv1.at[pl.ds(1, 2)], self.into + 1)

        def settled(self, by, half):
            s = step(place[1 - self.axis], by)
            passed, plain = self.rcv1[2, half, s], self.rcv1[1, 1 - half, s]
            return self.part[s, half] + passed.astype(jnp.float32) + plain.astype(jnp.float32)

        def out2(self):
            for way in range(2):
                self.snd2[way] = encode(self.settled(2, way))
                to = along(1 - self.axis, 1 + 2 * way)
                send(self.snd2.at[way], self.rcv2.at[way], self.out + 1, self.into + 2, to)

        def go2(self, way, kind, half):
            across = (half - zh) * (half - zh)
            to = along(1 - self.axis, 1 + 2 * way, step(z, 2 * across))
            src = self.snd2.at[2 * kind + way]
            send(src, self.rcv2.at[2 * kind + across], self.out + 1, self.into + 3, to)

        def beside2(self):
            for way in range(2):
                self.snd2[2 + way] = encode(self.settled(1 + 2 * way, 1 - way))
                self.go2(way, 1, 1 - way)
            self.snd2[6] = encode(self.settled(0, 1 - zh))
            send(self.snd2.at[6], self.rcv2.at[6], self.out + 1, self.into + 3, dev(y, x, far, core))

        def relay2(self):
            values = [self.settled(1 + 2 * way, way) for way in range(2)]
            arrived(self.rcv2.at[pl.ds(0, 2)], self.into + 2)
            for way in range(2):
                self.snd2[4 + way] = encode(values[way] + decode(self.rcv2[way]))
                self.go2(way, 2, way)

        def end2(self):
            mine = self.settled(0, zh)
            arrived(self.rcv2.at[pl.ds(2, 5)], self.into + 3)
            out_ref[:, self.at : self.at + self.width] = mine + sum(decode(self.rcv2[slot]) for slot in range(2, 7))

        def out_straight(self):
            for across in (0, 1):
                for by in (2, 1, 3, 0):
                    if by or across:
                        slot = 2 * by + across - 1
                        self.snd2[slot] = encode(self.settled(by, zh + across * (1 - 2 * zh)))
                        to = along(1 - self.axis, by, far if across else z)
                        send(self.snd2.at[slot], self.rcv2.at[slot], self.out + 1, self.into + 2, to)

        def end_straight(self):
            mine = self.settled(0, zh)
            arrived(self.rcv2, self.into + 2)
            out_ref[:, self.at : self.at + self.width] = mine + sum(decode(self.rcv2[slot]) for slot in range(7))

    a0, b0, a1, b1 = (Ring(n) for n in range(4))

    respond(0)
    a0.early(early.at[0])
    b0.early(early.at[1])
    respond(1)
    a0.far(early.at[0])
    a0.go1(0)
    b0.far(early.at[1])
    b0.go1(0)
    for r in (a0, b0):
        r.beside()
    for r in (a0, b0):
        r.own()
    for r in (a1, b1):
        r.far()
    for r in (a0, b0):
        r.relay1()
    for r in (a1, b1):
        r.go1(0)
    for r in (a1, b1):
        r.beside()
        r.own()
    left(rows.at[pl.ds(0, 6)], ROWS_OUT)
    left(st_in, STATS_OUT)
    for r in (a0, b0):
        r.arrive1()
        r.out2()
    for r in (a1, b1):
        r.relay1()
    for r in (a0, b0):
        r.beside2()
    for r in (a0, b0):
        r.relay2()
    for r in (a1, b1):
        r.arrive1()
        r.out_straight()
    for r in (a0, b0, a1, b1):
        left(r.snd1, r.out)
    for r in (a0, b0):
        left(r.snd2, r.out + 1)
    for r in (a0, b0):
        r.end2()
    for r in (a1, b1):
        r.end_straight()

    total = out_ref[...]
    norm = lax.rsqrt(jnp.sum(total * total, axis=1, keepdims=True) * (1.0 / D) + 1e-06)
    out_ref[...] = total * norm
    for r in (a1, b1):
        left(r.snd2, r.out + 1)


def ring_buffers(width):
    f32, bf16 = jnp.float32, jnp.bfloat16
    second = pltpu.VMEM((7, 32, width), bf16)
    return [
        pltpu.VMEM((3, 2, 4, 32, width), bf16),
        pltpu.VMEM((3, 2, 4, 32, width), bf16),
        pltpu.VMEM((2, 4, 32, width), f32),
        pltpu.VMEM((4, 2, 32, width), f32),
        second,
        second,
    ]


def per_device(embeddings, centroids):
    f32, bf16 = jnp.float32, jnp.bfloat16
    return pl.pallas_call(
        kernel,
        out_shape=pltpu.VMEM((32, D), f32),
        in_specs=[pl.BlockSpec(memory_space=pl.ANY)] * 2,
        out_specs=pl.BlockSpec(memory_space=pltpu.VMEM),
        scratch_shapes=[
            pltpu.VMEM((KB, D), bf16),
            pltpu.VMEM((8, 128, D), bf16),
            pltpu.VMEM((4, KB, 256), f32),
            pltpu.VMEM((KB, 4 * ROWS), bf16),
            pltpu.VMEM((8, 4 * ROWS), f32),
            pltpu.VMEM((2, 4, 8, 128), f32),
            pltpu.VMEM((2, 3, 4, 8, 128), f32),
            pltpu.VMEM((2, 256, 512), f32),
            [ring_buffers(width) for width in WIDTHS],
            pltpu.SemaphoreType.DMA((3,)),
            pltpu.SemaphoreType.DMA((N_SEND,)),
            pltpu.SemaphoreType.DMA((N_RECEIVE,)),
        ],
        compiler_params=pltpu.CompilerParams(collective_id=0, has_side_effects=True, vmem_limit_bytes=60 * 1024 * 1024),
        cost_estimate=pl.CostEstimate(flops=4 * KB * 4 * ROWS * D, bytes_accessed=5 * 1024 * 1024, transcendentals=KB * KB),
    )(embeddings, centroids)


def solution(mesh):
    placed = (P(("img", "cen"), None), P("cen", None))
    return jax.shard_map(per_device, mesh=mesh, in_specs=placed, out_specs=P(("cen", "img"), None), check_vma=False)
```
